32 devices in a mesh: group: 2 (over y), role: 2 (over x), tp: 4 (over z), sub: 2 (over core).
Axes of the slice: x: 2, y: 2, z: 4, core: 2. Of those that a mesh axis runs over, the one named last changes fastest.
Arguments:
- residual: bfloat16 [128, 3072], P(('group', 'role', 'tp', 'sub')), parts along dimension 0, may hold values from -12 to 12
- query: bfloat16 [128, 3072], P(('group', 'role', 'tp', 'sub')), parts along dimension 0, may hold values from -6 to 6
- new_key: bfloat16 [128, 1024], P(('group', 'role', 'tp', 'sub')), parts along dimension 0, may hold values from -6 to 6
- new_value: bfloat16 [128, 1024], P(('group', 'role', 'tp', 'sub')), parts along dimension 0, may hold values from -6 to 6
- cache_key: bfloat16 [128, 128, 1024], P(('group', 'role', 'tp', 'sub')), parts along dimension 0, may hold values from -6 to 6
- cache_value: bfloat16 [128, 128, 1024], P(('group', 'role', 'tp', 'sub')), parts along dimension 0, may hold values from -6 to 6
- lengths: int32 [128], P(('group', 'role', 'tp', 'sub')), parts along dimension 0, may hold values from 2 to 128, as said below
- norm_gain: float32 [3072], replicated, may hold values from 0.1 to 1.9
- expert_ids: int32 [128, 2], P(('group', 'role', 'tp', 'sub')), parts along dimension 0, may hold values from 0 to 3, all different within a row; in each aligned block of 4 rows (0 to 3, 4 to 7, ...) at most 3 rows name the same one
- gate_levels: int32 [128, 2], P(('group', 'role', 'tp', 'sub')), parts along dimension 0, may hold values from 1 to 255
- gate_codes: bfloat16 [4, 3072, 8192], P('role', 'sub', 'tp'), may hold values from -7.5 to 7.5, as said below
- gate_scales: float32 [4, 24, 64], P('role', 'sub', 'tp'), may hold values from 0.0018042196 to 0.010825317
- up_codes: bfloat16 [4, 3072, 8192], P('role', 'sub', 'tp'), may hold values from -7.5 to 7.5, as said below
- up_scales: float32 [4, 24, 64], P('role', 'sub', 'tp'), may hold values from 0.0018042196 to 0.010825317
- down_codes: bfloat16 [4, 8192, 3072], P('role', 'tp', 'sub'), may hold values from -7.5 to 7.5, as said below
- down_scales: float32 [4, 64, 24], P('role', 'tp', 'sub'), may hold values from 0.0022097088 to 0.013258252
Outputs:
- mixed: bfloat16 [128, 3072], P(('group', 'role', 'tp', 'sub')), parts along dimension 0
The draws below stay inside these ranges and needn't reach their ends.
There are 2 independent parts, one for each index of `group`. The reference program is written for one: setup_inputs(seed, part) draws one part's arguments, and reference() takes and returns one part's arrays. A program takes and returns all parts, laid end to end along the dimension named above; an argument that names none is the same for every part. Nothing has to cross between parts.
Inputs may be any that keep to these rules, and one draw needn't show every extreme that they name: The first lengths[r] positions of row r's cache are filled; the first row of every part fills all 128. `expert_ids`: a row's two ids differ; among the rows of one device no expert is named by more than 3 rows, and some device has an expert named by exactly 3. `gate_codes`: each entry is s * 2 ** k * (1 + m / 8) with sign s, whole k from -2 to 2 and whole m from 0 to 7. `up_codes`: each entry is s * 2 ** k * (1 + m / 8) with sign s, whole k from -2 to 2 and whole m from 0 to 7. `down_codes`: each entry is s * 2 ** k * (1 + m / 8) with sign s, whole k from -2 to 2 and whole m from 0 to 7.
All inputs are finite; a program needn't handle non-finite values.
Results may differ from the reference program's by a relative error of at most 0.014.
Values may be sent and summed in bfloat16 or wider, within the bound.
No kernel may reach another device: no remote copies, remote signals or barrier semaphores. Data moves between devices by JAX's collectives and lax.ppermute only.
A program may use at most 192 MiB of HBM per device.

```python
import math
import jax
import jax.numpy as jnp
import numpy as np
from jax import lax

D = 3072
HEADS = 24
KV_HEADS = 8
HEAD_DIM = 128
FF = 8192
EXPERTS = 4
QBLOCK = 128
ROWS_DEV = 4
CACHE = 128
CAP = 3
ROWS = 64
N_TP = 4


def code_grid(key, shape):
    drawn = jax.random.randint(key, shape, 0, 80)
    powers = jnp.array([0.25, 0.5, 1.0, 2.0, 4.0], jnp.float32)
    magnitude = powers[drawn // 16] * (1.0 + (drawn // 2 % 8).astype(jnp.float32) / 8.0)
    signs = (drawn % 2 * 2 - 1).astype(jnp.float32)
    return (signs * magnitude).astype(jnp.bfloat16)


def draw_query(key, part):
    key = jax.random.fold_in(key, 11)
    values = jax.random.normal(key, (ROWS, D), jnp.float32)
    return jnp.clip(values, -6.0, 6.0).astype(jnp.bfloat16)


def draw_cache_key(key, part):
    key = jax.random.fold_in(key, 12)
    shape = (ROWS, CACHE, KV_HEADS, HEAD_DIM)
    values = jax.random.normal(key, shape, jnp.float32)
    values = jnp.clip(values, -6.0, 6.0)
    return values.reshape(ROWS, CACHE, KV_HEADS * HEAD_DIM).astype(jnp.bfloat16)


def draw_residual(key, part):
    key = jax.random.fold_in(key, 13)
    value_key, column_key = jax.random.split(key, 2)
    columns = jnp.exp(jax.random.uniform(column_key, (D,), jnp.float32, 0.0, math.log(10.0))) / 3.0
    values = jax.random.normal(value_key, (ROWS, D), jnp.float32) * columns[None, :]
    return jnp.clip(values, -12.0, 12.0).astype(jnp.bfloat16)


def draw_lengths(key, part):
    key = jax.random.fold_in(key, 31)
    drawn = jax.random.randint(key, (ROWS,), 2, CACHE + 1)
    return drawn.at[0].set(CACHE).astype(jnp.int32)


def draw_gate_codes(key, part):
    key = jax.random.fold_in(key, 21)
    return code_grid(key, (EXPERTS, D, FF))


def draw_up_codes(key, part):
    key = jax.random.fold_in(key, 22)
    return code_grid(key, (EXPERTS, D, FF))


def draw_down_codes(key, part):
    key = jax.random.fold_in(key, 23)
    return code_grid(key, (EXPERTS, FF, D))


def plant(entries, key, low, top_value):
    longest = entries.shape.index(max(entries.shape))
    spots = []
    for shift in (0, 1):
        where = [jax.random.randint(jax.random.fold_in(key, axis), (), 0, length) for axis, length in enumerate(entries.shape)]
        where[longest] = (where[longest] + shift) % entries.shape[longest]
        spots.append(tuple(where))
    return entries.at[spots[0]].set(low).at[spots[1]].set(top_value)


def shard_levels(rng, extent, cuts, low, largest):
    def one(axis_at, parts):
        steps = jax.random.uniform(jax.random.fold_in(jax.random.fold_in(rng, 6), axis_at), (parts,), jnp.float32, low / len(cuts), largest / len(cuts))
        return jnp.repeat(jnp.exp(steps), extent[axis_at] // parts).reshape((-1,) + (1,) * (len(extent) - axis_at - 1))

    gain = one(*cuts[0])
    for cut in cuts[1:]:
        gain = gain * one(*cut)
    return gain


def routed_block(own_key, own, number, rows, number_of, top, bound, skew):
    order = jax.random.permutation(own_key, number_of)
    heavy_load, usual = portions_of(number_of, rows * top, bound, skew, True), portions_of(number_of, rows * top, bound, skew, False)
    places = jnp.arange(number_of)

    def named(sizes, turn):
        used = int((sizes > 0).sum())
        fixed = max(1, used // 4)
        moved = fixed + (places - fixed + turn * (used - fixed)) % max(1, number_of - fixed)
        return jnp.zeros((number_of,), jnp.int32).at[order[jnp.where(places < fixed, places, moved)]].set(jnp.asarray(sizes, jnp.int32))

    sizes = jnp.where(number % 4 == 0, named(heavy_load, number // 4), named(usual, number - number // 4 - 1))
    mixed = jax.random.permutation(jax.random.fold_in(own, 3), number_of)
    giver, receiver = mixed[0:number_of // 2 * 2:2], mixed[1:number_of // 2 * 2:2]
    slack = jnp.minimum(sizes[giver] - 1, bound - sizes[receiver]) // 2
    slack = jnp.where((giver == order[0]) | (receiver == order[0]) | (sizes[receiver] == 0), 0, jnp.maximum(slack, 0))
    moved = jax.random.randint(jax.random.fold_in(own, 4), (number_of // 2,), 0, 1 << 20) % (slack + 1)
    sizes = sizes.at[giver].add(-moved).at[receiver].add(moved)
    members = jnp.searchsorted(jnp.cumsum(sizes), jnp.arange(rows * top), side="right").astype(jnp.int32)
    table = members.reshape(top, rows).T
    table = table[jax.random.permutation(jax.random.fold_in(own, 1), rows)]
    turn = jax.random.randint(jax.random.fold_in(own, 2), (rows, 1), 0, top)
    return jnp.take_along_axis(table, (jnp.arange(top)[None, :] + turn) % top, axis=1)


def portions_of(count, total, reach, lean, full):
    loads = [(1 << 20) // math.isqrt(standing ** lean) + 1 for standing in range(1, count + 1)]
    largest = reach if full else min(reach, max(-(-total // count), total * loads[0] // sum(loads)))
    least = 1 if total - largest >= count - 1 else 0
    holding, rest = [largest] + [least] * (count - 1), total - largest - least * (count - 1)
    while rest > 0:
        movable = [i for i in range(1, count) if holding[i] < largest] or [i for i in range(1, count) if holding[i] < reach]
        whole, remaining = sum([loads[i] for i in movable]), rest
        for i in movable:
            more = min(reach - holding[i], max(1, remaining * loads[i] // whole), rest)
            holding[i] = holding[i] + more
            rest = rest - more
    return np.array(holding)


def bell_draw(own_key, extent, deviation, bound, pieces=(), held_as=jnp.bfloat16):
    values = jax.random.normal(own_key, extent, jnp.float32) * deviation
    if len(pieces) > 0:
        values = shard_levels(own_key, extent, pieces, -0.22, 0.18) * values
    return jnp.clip(values, min=-bound, max=bound).astype(held_as)


def setup_inputs(seed: int = 0, part: int = 0) -> dict:
    keys = jax.random.split(jax.random.key(seed), 17)
    part_splits = jax.random.split(jax.random.fold_in(keys[16], part), 17)
    residual = draw_residual(jax.random.fold_in(jax.random.fold_in(keys[16], part), 71), part)
    query = draw_query(jax.random.fold_in(jax.random.fold_in(keys[16], part), 71), part)
    new_key = bell_draw(part_splits[2], (ROWS, KV_HEADS * HEAD_DIM), 1.0, 6.0, ((0, 16),))
    new_value = bell_draw(part_splits[3], (ROWS, KV_HEADS * HEAD_DIM), 1.0, 6.0, ((0, 16),))
    cache_key = draw_cache_key(jax.random.fold_in(jax.random.fold_in(keys[16], part), 71), part)
    cache_value = bell_draw(part_splits[5], (ROWS, CACHE, KV_HEADS * HEAD_DIM), 1.0, 6.0, ((0, 16),))
    lengths = draw_lengths(jax.random.fold_in(jax.random.fold_in(keys[16], part), 71), part)
    norm_gain = jnp.clip(1.0 + 0.18 * jax.random.normal(keys[7], (D,), jnp.float32), 0.1, 1.9)
    expert_ids_keys = jax.random.split(jax.random.fold_in(part_splits[8], 1), ROWS // ROWS_DEV)
    expert_ids_turns = jax.random.permutation(jax.random.fold_in(part_splits[8], 3), ROWS // ROWS_DEV)
    expert_ids = jax.vmap(lambda own, number: routed_block(jax.random.fold_in(part_splits[8], 2), own, number, ROWS_DEV, EXPERTS, 2, CAP, 2))(expert_ids_keys, expert_ids_turns).reshape((ROWS, 2))
    gate_levels = plant(jax.random.randint(part_splits[9], (ROWS, 2), 1, 256), jax.random.fold_in(part_splits[9], 1), 1, 255).astype(jnp.int32)
    gate_codes = draw_gate_codes(jax.random.fold_in(keys[16], 71), part)
    gate_scales = jnp.clip(jnp.exp(math.log(0.010825317) - 1.7917595 * jax.random.uniform(keys[11], (EXPERTS, D // QBLOCK, FF // QBLOCK), jnp.float32) ** shard_levels(keys[11], (EXPERTS, D // QBLOCK, FF // QBLOCK), ((0, 2), (1, 2), (2, 4)), -0.2, 0.2)), 0.0018042196, 0.010825317)
    up_codes = draw_up_codes(jax.random.fold_in(keys[16], 71), part)
    up_scales = jnp.clip(jnp.exp(math.log(0.010825317) - 1.7917595 * jax.random.uniform(keys[13], (EXPERTS, D // QBLOCK, FF // QBLOCK), jnp.float32) ** shard_levels(keys[13], (EXPERTS, D // QBLOCK, FF // QBLOCK), ((0, 2), (1, 2), (2, 4)), -0.2, 0.2)), 0.0018042196, 0.010825317)
    down_codes = draw_down_codes(jax.random.fold_in(keys[16], 71), part)
    down_scales = jnp.clip(jnp.exp(math.log(0.013258252) - 1.7917594341056822 * jax.random.uniform(keys[15], (EXPERTS, FF // QBLOCK, D // QBLOCK), jnp.float32) ** shard_levels(keys[15], (EXPERTS, FF // QBLOCK, D // QBLOCK), ((0, 2), (1, 4), (2, 2)), -0.2, 0.2)), 0.0022097088, 0.013258252)
    return {"residual": residual, "query": query, "new_key": new_key, "new_value": new_value, "cache_key": cache_key, "cache_value": cache_value, "lengths": lengths, "norm_gain": norm_gain, "expert_ids": expert_ids, "gate_levels": gate_levels, "gate_codes": gate_codes, "gate_scales": gate_scales, "up_codes": up_codes, "up_scales": up_scales, "down_codes": down_codes, "down_scales": down_scales}


def dequantize(codes, scales):
    experts, rows, columns = codes.shape
    widened = jnp.repeat(scales, QBLOCK, axis=-1)
    blocked = codes.astype(jnp.float32).reshape(experts, rows // QBLOCK, QBLOCK, columns)
    return (blocked * widened[:, :, None, :]).reshape(experts, rows, columns).astype(jnp.bfloat16)

def attend(query, new_key, new_value, cache_key, cache_value, lengths):
    row_count = query.shape[0]
    positions = cache_key.shape[1]
    group_size = HEADS // KV_HEADS
    queries = query.astype(jnp.float32).reshape(row_count, KV_HEADS, group_size, HEAD_DIM)
    cache_keys = cache_key.astype(jnp.float32).reshape(row_count, positions, KV_HEADS, HEAD_DIM)
    cache_values = cache_value.astype(jnp.float32).reshape(row_count, positions, KV_HEADS, HEAD_DIM)
    fresh_key = new_key.astype(jnp.float32).reshape(row_count, KV_HEADS, HEAD_DIM)
    fresh_value = new_value.astype(jnp.float32).reshape(row_count, KV_HEADS, HEAD_DIM)
    factor = 1.0 / math.sqrt(HEAD_DIM)
    scores = jnp.einsum('rkgd,rpkd->rkgp', queries, cache_keys) * factor
    fresh_score = jnp.einsum('rkgd,rkd->rkg', queries, fresh_key) * factor
    valid_mask = lax.broadcasted_iota(jnp.int32, (row_count, positions), 1) < lengths[:, None]
    valid_mask = valid_mask[:, None, None, :]
    masked = jnp.where(valid_mask, scores, -1e+30)
    peak_score = jnp.maximum(lax.optimization_barrier(jnp.max(masked, axis=-1)), fresh_score)
    exp_scores = jnp.where(valid_mask, jnp.exp(masked - peak_score[..., None]), 0.0)
    fresh_exp = jnp.exp(fresh_score - peak_score)
    denominator = lax.optimization_barrier(jnp.sum(exp_scores, axis=-1)) + fresh_exp
    probabilities = (exp_scores / denominator[..., None]).astype(jnp.bfloat16)
    fresh_prob = (fresh_exp / denominator).astype(jnp.bfloat16)
    attended = jnp.einsum('rkgp,rpkd->rkgd', probabilities.astype(jnp.float32), cache_values)
    attended = attended + fresh_prob.astype(jnp.float32)[..., None] * fresh_value[:, :, None, :]
    return attended.reshape(row_count, D)

def reference(residual, query, new_key, new_value, cache_key, cache_value, lengths, norm_gain, expert_ids, gate_levels, gate_codes, gate_scales, up_codes, up_scales, down_codes, down_scales):
    stream = residual.astype(jnp.float32) + attend(query, new_key, new_value, cache_key, cache_value, lengths)
    mean_square = lax.optimization_barrier(jnp.mean(stream * stream, axis=1, keepdims=True))
    normed = (stream * lax.rsqrt(mean_square + 1e-05) * norm_gain).astype(jnp.bfloat16)

    def one_expert(tables):
        gate_c, gate_s, up_c, up_s, down_c, down_s = tables
        w_gate = dequantize(gate_c[None], gate_s[None])[0]
        w_up = dequantize(up_c[None], up_s[None])[0]
        w_down = dequantize(down_c[None], down_s[None])[0]
        gate_part = jnp.dot(normed, w_gate, preferred_element_type=jnp.float32)
        up_part = jnp.dot(normed, w_up, preferred_element_type=jnp.float32)
        hidden = (jax.nn.silu(gate_part) * up_part).astype(jnp.bfloat16)
        block_units = FF // N_TP
        hidden_blocks = hidden.astype(jnp.float32).reshape(ROWS, N_TP, block_units)
        down_blocks = w_down.astype(jnp.float32).reshape(N_TP, block_units, D)
        partial_value = jnp.einsum('rtf,tfd->rtd', hidden_blocks, down_blocks).astype(jnp.bfloat16)
        partial_value = lax.optimization_barrier(partial_value)
        return lax.optimization_barrier(jnp.sum(partial_value.astype(jnp.float32), axis=1)).astype(jnp.bfloat16)
    expert_outs = lax.map(one_expert, (gate_codes, gate_scales, up_codes, up_scales, down_codes, down_scales))
    levels = gate_levels.astype(jnp.float32)
    shares = levels / lax.optimization_barrier(jnp.sum(levels, axis=1, keepdims=True))
    picked = (expert_ids[:, :, None] == jnp.arange(EXPERTS, dtype=jnp.int32)[None, None, :]).astype(jnp.float32)
    coefficient = lax.optimization_barrier(jnp.sum(picked * shares[:, :, None], axis=1))
    expert_sum = jnp.einsum('re,erd->rd', coefficient, expert_outs.astype(jnp.float32))
    return (stream + expert_sum).astype(jnp.bfloat16)
```

```python
import functools
import math

import jax
import jax.numpy as jnp
from jax import lax
from jax.experimental import pallas as pl
from jax.experimental.pallas import tpu as pltpu
from jax.sharding import PartitionSpec as P

D = 3072
HEADS = 24
KV_HEADS = 8
HEAD_DIM = 128
EXPERTS = 4
QBLOCK = 128
LANES = 128
GROUP = HEADS // KV_HEADS
SLOT = 16
VMEM_LIMIT = 16 << 20
COST = 48 << 20

VMEM = pl.BlockSpec(memory_space=pltpu.VMEM)
SMEM = pl.BlockSpec(memory_space=pltpu.SMEM)


def attend_kernel(
    residual_ref,
    query_ref,
    new_key_ref,
    new_value_ref,
    cache_key_ref,
    cache_value_ref,
    lengths_ref,
    gain_ref,
    ids_ref,
    levels_ref,
    own_ref,
    other_ref,
    stream_ref,
    q_scr,
    nk_scr,
    nv_scr,
    att_scr,
):
    rows, positions, _ = cache_key_ref.shape
    half = D // 2
    f32 = jnp.float32
    total = KV_HEADS * SLOT
    zeros = jnp.zeros((total, HEAD_DIM), f32)
    q_scr[...] = zeros
    nk_scr[...] = zeros
    nv_scr[...] = zeros
    for j in range(KV_HEADS):
        kv_cols = slice(j * HEAD_DIM, (j + 1) * HEAD_DIM)
        fresh_key = new_key_ref[:, kv_cols].astype(f32)
        fresh_value = new_value_ref[:, kv_cols].astype(f32)
        for g in range(GROUP):
            h = j * GROUP + g
            at = slice(j * SLOT + g * rows, j * SLOT + (g + 1) * rows)
            q_scr[at, :] = query_ref[:, h * HEAD_DIM : (h + 1) * HEAD_DIM].astype(f32)
            nk_scr[at, :] = fresh_key
            nv_scr[at, :] = fresh_value
    queries = q_scr[...]
    factor = 1.0 / math.sqrt(HEAD_DIM)
    fresh_score = jnp.sum(queries * nk_scr[...], axis=1, keepdims=True) * factor
    queries_bf = queries.astype(jnp.bfloat16)
    keys = cache_key_ref[...].reshape(rows * positions, KV_HEADS * HEAD_DIM)
    values = cache_value_ref[...].reshape(rows * positions, KV_HEADS * HEAD_DIM)
    scores = jnp.concatenate(
        [
            lax.dot_general(
                queries_bf[j * SLOT : (j + 1) * SLOT],
                keys[:, j * HEAD_DIM : (j + 1) * HEAD_DIM],
                (((1,), (1,)), ((), ())),
                preferred_element_type=f32,
            )
            for j in range(KV_HEADS)
        ],
        axis=0,
    )
    row_of = lax.broadcasted_iota(jnp.int32, (total, positions), 0) % rows
    position = lax.broadcasted_iota(jnp.int32, (total, positions), 1)
    valid = [
        jnp.logical_and(row_of == r, position < lengths_ref[r]) for r in range(rows)
    ]
    pieces = [
        jnp.where(valid[r], scores[:, r * positions : (r + 1) * positions] * factor, -1e30)
        for r in range(rows)
    ]
    peak = functools.reduce(jnp.maximum, pieces)
    peak = jnp.maximum(jnp.max(peak, axis=1, keepdims=True), fresh_score)
    exps = [jnp.where(valid[r], jnp.exp(pieces[r] - peak), 0.0) for r in range(rows)]
    fresh_exp = jnp.exp(fresh_score - peak)
    denominator = jnp.sum(sum(exps[1:], exps[0]), axis=1, keepdims=True) + fresh_exp
    inverse = 1.0 / denominator
    probabilities = jnp.concatenate([(e * inverse).astype(jnp.bfloat16) for e in exps], axis=1)
    fresh_prob = (fresh_exp * inverse).astype(jnp.bfloat16).astype(f32)
    attended = jnp.concatenate(
        [
            jnp.dot(
                probabilities[j * SLOT : (j + 1) * SLOT],
                values[:, j * HEAD_DIM : (j + 1) * HEAD_DIM],
                preferred_element_type=f32,
            )
            for j in range(KV_HEADS)
        ],
        axis=0,
    )
    att_scr[...] = attended + fresh_prob * nv_scr[...]
    squares = jnp.zeros((rows, HEAD_DIM), f32)
    for j in range(KV_HEADS):
        for g in range(GROUP):
            h = j * GROUP + g
            cols = slice(h * HEAD_DIM, (h + 1) * HEAD_DIM)
            at = slice(j * SLOT + g * rows, j * SLOT + (g + 1) * rows)
            piece = residual_ref[:, cols].astype(f32) + att_scr[at, :]
            stream_ref[:, cols] = piece
            squares = squares + piece * piece
    mean_square = jnp.sum(squares, axis=1, keepdims=True) * (1.0 / D)
    normed = stream_ref[...] * lax.rsqrt(mean_square + 1e-05) * gain_ref[...]
    first = lax.axis_index("sub") == 0
    low, high = normed[:, :half], normed[:, half:]
    lane = lax.broadcasted_iota(jnp.int32, (rows, LANES), 1)
    levels = levels_ref[...].astype(f32)
    ids = ids_ref[...]
    table = jnp.where(lane == ids[:, 0:1], levels[:, 0:1], 0.0) + jnp.where(
        lane == ids[:, 1:2], levels[:, 1:2], 0.0
    )
    own = jnp.concatenate([jnp.where(first, low, high), table], axis=1)
    other = jnp.concatenate([jnp.where(first, high, low), table], axis=1)
    for ref, value in ((own_ref, own), (other_ref, other)):
        ref[...] = jnp.concatenate(
            [jnp.where(first, value, 0.0), jnp.where(first, 0.0, value)], axis=0
        ).astype(jnp.bfloat16)


def scaled_product(left, weights_ref, scales_ref, expert, column, width):
    depth = weights_ref.shape[1]
    total = None
    for k in range(depth // QBLOCK):
        product = jnp.dot(
            left[:, k * QBLOCK : (k + 1) * QBLOCK],
            weights_ref[expert, k * QBLOCK : (k + 1) * QBLOCK, column : column + width],
            preferred_element_type=jnp.float32,
        )
        product = jnp.concatenate(
            [
                product[:, i * QBLOCK : (i + 1) * QBLOCK]
                * scales_ref[expert, k, column // QBLOCK + i]
                for i in range(width // QBLOCK)
            ],
            axis=1,
        )
        total = product if total is None else total + product
    return total


def gate_up_kernel(x_ref, gate_ref, up_ref, gate_s_ref, up_s_ref, out_ref, *, expert):
    _, depth, units = gate_ref.shape
    rows = x_ref.shape[0]
    block = min(rows, 64)
    width = 256
    for m in range(rows // block):
        at = slice(m * block, (m + 1) * block)
        left = x_ref[at, :depth]
        for column in range(0, units, width):
            out_ref[at, column : column + width] = scaled_product(
                left, gate_ref, gate_s_ref, expert, column, width
            ).astype(jnp.bfloat16)
            out_ref[at, units + column : units + column + width] = scaled_product(
                left, up_ref, up_s_ref, expert, column, width
            ).astype(jnp.bfloat16)


def down_kernel(x_ref, *refs, experts):
    parts = refs[: 2 * experts]
    down_ref, down_s_ref, out_ref = refs[2 * experts :]
    _, units, columns = down_ref.shape
    rows, extended = x_ref.shape
    block = min(rows, 64)
    width = 256
    f32 = jnp.float32
    base = lax.axis_index("role") * experts
    for m in range(rows // block):
        at = slice(m * block, (m + 1) * block)
        levels = x_ref[at, extended - LANES :].astype(f32)
        lane = lax.broadcasted_iota(jnp.int32, levels.shape, 1)
        shares = levels / jnp.sum(levels, axis=1, keepdims=True)
        hidden = []
        for e in range(experts):
            share = jnp.sum(jnp.where(lane == base + e, shares, 0.0), axis=1, keepdims=True)
            mine, theirs = parts[2 * e], parts[2 * e + 1]
            chunks = []
            for u in range(0, units, width):
                gate = mine[at, u : u + width].astype(f32) + theirs[at, u : u + width].astype(f32)
                v = slice(units + u, units + u + width)
                up = mine[at, v].astype(f32) + theirs[at, v].astype(f32)
                silu = gate / (1.0 + jnp.exp(-gate))
                chunks.append((silu * up * share).astype(jnp.bfloat16))
            hidden.append(jnp.concatenate(chunks, axis=1))
        for column in range(0, columns, width):
            total = None
            for e in range(experts):
                product = scaled_product(hidden[e], down_ref, down_s_ref, e, column, width)
                total = product if total is None else total + product
            out_ref[at, column : column + width] = total.astype(jnp.bfloat16)


def finish_kernel(stream_ref, own_ref, other_ref, out_ref):
    half = D // 2
    rows = stream_ref.shape[0]
    first = lax.axis_index("sub") == 0
    own, other = (
        jnp.where(first, pair[:rows], pair[rows:])
        for pair in (own_ref[...].astype(jnp.float32), other_ref[...].astype(jnp.float32))
    )
    out_ref[:, :half] = (stream_ref[:, :half] + jnp.where(first, own, other)).astype(jnp.bfloat16)
    out_ref[:, half:] = (stream_ref[:, half:] + jnp.where(first, other, own)).astype(jnp.bfloat16)


def swap(x, axis, bit):
    count = lax.axis_size(axis)
    return lax.ppermute(x, axis, [(i, i ^ bit) for i in range(count)])


def bits(axis):
    return [1 << b for b in range(lax.axis_size(axis).bit_length() - 1)]


def add_bf16(a, b):
    return (a.astype(jnp.float32) + b.astype(jnp.float32)).astype(jnp.bfloat16)


def per_device(
    residual,
    query,
    new_key,
    new_value,
    cache_key,
    cache_value,
    lengths,
    norm_gain,
    expert_ids,
    gate_levels,
    gate_codes,
    gate_scales,
    up_codes,
    up_scales,
    down_codes,
    down_scales,
):
    rows = residual.shape[0]
    half = D // 2
    extended = half + LANES
    params = pltpu.CompilerParams(vmem_limit_bytes=VMEM_LIMIT)
    cost = pl.CostEstimate(flops=0, bytes_accessed=COST, transcendentals=0)
    stacked = pltpu.VMEM((KV_HEADS * SLOT, HEAD_DIM), jnp.float32)
    own, other, stream = pl.pallas_call(
        attend_kernel,
        out_shape=(
            jax.ShapeDtypeStruct((2 * rows, extended), jnp.bfloat16),
            jax.ShapeDtypeStruct((2 * rows, extended), jnp.bfloat16),
            jax.ShapeDtypeStruct((rows, D), jnp.float32),
        ),
        in_specs=[VMEM] * 6 + [SMEM] + [VMEM] * 3,
        out_specs=(VMEM, VMEM, VMEM),
        scratch_shapes=[stacked] * 4,
        compiler_params=params,
        cost_estimate=cost,
        name="attend",
    )(
        residual,
        query,
        new_key,
        new_value,
        cache_key,
        cache_value,
        lengths,
        norm_gain.reshape(1, D),
        expert_ids,
        gate_levels,
    )
    gathered = own + swap(other, "sub", 1)
    steps = [("tp", bit) for bit in bits("tp")] + [("role", bit) for bit in bits("role")]
    for axis, bit in steps:
        gathered = jnp.concatenate([gathered, swap(gathered, axis, bit)], axis=0)
    total_rows = gathered.shape[0]
    experts, _, units = gate_codes.shape
    parts = []
    for e in range(experts):
        part = pl.pallas_call(
            functools.partial(gate_up_kernel, expert=e),
            out_shape=jax.ShapeDtypeStruct((total_rows, 2 * units), jnp.bfloat16),
            in_specs=[VMEM] * 3 + [SMEM] * 2,
            out_specs=VMEM,
            compiler_params=params,
            name="gate_up",
        )(gathered, gate_codes, up_codes, gate_scales, up_scales)
        parts += [part, swap(part, "sub", 1)]
    carried = pl.pallas_call(
        functools.partial(down_kernel, experts=experts),
        out_shape=jax.ShapeDtypeStruct((total_rows, half), jnp.bfloat16),
        in_specs=[VMEM] * (2 + 2 * experts) + [SMEM],
        out_specs=VMEM,
        compiler_params=params,
        name="down",
    )(gathered, *parts, down_codes, down_scales)
    for axis, bit in reversed(steps):
        kept = carried.shape[0] // 2
        carried = add_bf16(carried[:kept], swap(carried[kept:], axis, bit))
    return pl.pallas_call(
        finish_kernel,
        out_shape=jax.ShapeDtypeStruct((rows, D), jnp.bfloat16),
        in_specs=[VMEM] * 3,
        out_specs=VMEM,
        compiler_params=params,
        name="finish",
    )(stream, carried, swap(carried, "sub", 1))


def solution(mesh):
    row = ("group", "role", "tp", "sub")
    in_specs = (
        P(row, None),
        P(row, None),
        P(row, None),
        P(row, None),
        P(row, None, None),
        P(row, None, None),
        P(row),
        P(),
        P(row, None),
        P(row, None),
        P("role", "sub", "tp"),
        P("role", "sub", "tp"),
        P("role", "sub", "tp"),
        P("role", "sub", "tp"),
        P("role", "tp", "sub"),
        P("role", "tp", "sub"),
    )
    return jax.shard_map(
        per_device, mesh=mesh, in_specs=in_specs, out_specs=P(row, None), check_vma=False
    )
```

```python
import functools
import math

import jax
import jax.numpy as jnp
from jax import lax
from jax.experimental import pallas as pl
from jax.experimental.pallas import tpu as pltpu
from jax.sharding import PartitionSpec as P

D = 3072
HEADS = 24
KV_HEADS = 8
HEAD_DIM = 128
EXPERTS = 4
QBLOCK = 128
LANES = 128
GROUP = HEADS // KV_HEADS
SLOT = 16
PIECES = 2
VMEM_LIMIT = 16 << 20

LOAD_ATTEND = 1
LOAD_STEP = (2, 2, 2)
LOAD_GATE_UP = 2
LOAD_DOWN = 1
WIDTH = 512

VMEM = pl.BlockSpec(memory_space=pltpu.VMEM)
ANY = pl.BlockSpec(memory_space=pltpu.HBM)


def segment(ref, expert, piece):
    depth = ref.shape[1] // PIECES
    return ref.at[expert, pl.ds(piece * depth, depth), :]


def start_loads(places, sources, targets, sems):
    copies = [
        pltpu.make_async_copy(segment(source, *place), target, sems.at[i])
        for i, (place, source, target) in enumerate(zip(places, sources, targets))
    ]
    for copy in copies:
        copy.start()
    return copies


def attend_kernel(*refs, places):
    count = len(places)
    inputs = refs[:10]
    sources = refs[10 : 10 + count]
    own_ref, other_ref, stream_ref = refs[10 + count : 13 + count]
    targets = refs[13 + count : 13 + 2 * count]
    scratch = refs[13 + 2 * count :]
    held = scratch[:10]
    q_scr, nk_scr, nv_scr, att_scr, in_sems, load_sems = scratch[10:]
    copies = [
        pltpu.make_async_copy(source, target, in_sems.at[i])
        for i, (source, target) in enumerate(zip(inputs, held))
    ]
    for copy in copies:
        copy.start()
    loads = start_loads(places, sources, targets, load_sems)
    (
        query_ref,
        new_key_ref,
        new_value_ref,
        lengths_ref,
        cache_key_ref,
        cache_value_ref,
        residual_ref,
        gain_ref,
        ids_ref,
        levels_ref,
    ) = held
    for copy in copies[:4]:
        copy.wait()
    rows, positions, _ = cache_key_ref.shape
    half = D // 2
    f32 = jnp.float32
    total = KV_HEADS * SLOT
    zeros = jnp.zeros((total, HEAD_DIM), f32)
    q_scr[...] = zeros
    nk_scr[...] = zeros
    nv_scr[...] = zeros
    for j in range(KV_HEADS):
        kv_cols = slice(j * HEAD_DIM, (j + 1) * HEAD_DIM)
        fresh_key = new_key_ref[:, kv_cols].astype(f32)
        fresh_value = new_value_ref[:, kv_cols].astype(f32)
        for g in range(GROUP):
            h = j * GROUP + g
            at = slice(j * SLOT + g * rows, j * SLOT + (g + 1) * rows)
            q_scr[at, :] = query_ref[:, h * HEAD_DIM : (h + 1) * HEAD_DIM].astype(f32)
            nk_scr[at, :] = fresh_key
            nv_scr[at, :] = fresh_value
    queries = q_scr[...]
    factor = 1.0 / math.sqrt(HEAD_DIM)
    fresh_score = jnp.sum(queries * nk_scr[...], axis=1, keepdims=True) * factor
    queries_bf = queries.astype(jnp.bfloat16)
    copies[4].wait()
    keys = cache_key_ref[...].reshape(rows * positions, KV_HEADS * HEAD_DIM)
    scores = jnp.concatenate(
        [
            lax.dot_general(
                queries_bf[j * SLOT : (j + 1) * SLOT],
                keys[:, j * HEAD_DIM : (j + 1) * HEAD_DIM],
                (((1,), (1,)), ((), ())),
                preferred_element_type=f32,
            )
            for j in range(KV_HEADS)
        ],
        axis=0,
    )
    row_of = lax.broadcasted_iota(jnp.int32, (total, positions), 0) % rows
    position = lax.broadcasted_iota(jnp.int32, (total, positions), 1)
    valid = [
        jnp.logical_and(row_of == r, position < lengths_ref[r]) for r in range(rows)
    ]
    pieces = [
        jnp.where(valid[r], scores[:, r * positions : (r + 1) * positions] * factor, -1e30)
        for r in range(rows)
    ]
    peak = functools.reduce(jnp.maximum, pieces)
    peak = jnp.maximum(jnp.max(peak, axis=1, keepdims=True), fresh_score)
    exps = [jnp.where(valid[r], jnp.exp(pieces[r] - peak), 0.0) for r in range(rows)]
    fresh_exp = jnp.exp(fresh_score - peak)
    denominator = jnp.sum(sum(exps[1:], exps[0]), axis=1, keepdims=True) + fresh_exp
    inverse = 1.0 / denominator
    probabilities = jnp.concatenate([(e * inverse).astype(jnp.bfloat16) for e in exps], axis=1)
    fresh_prob = (fresh_exp * inverse).astype(jnp.bfloat16).astype(f32)
    copies[5].wait()
    values = cache_value_ref[...].reshape(rows * positions, KV_HEADS * HEAD_DIM)
    attended = jnp.concatenate(
        [
            jnp.dot(
                probabilities[j * SLOT : (j + 1) * SLOT],
                values[:, j * HEAD_DIM : (j + 1) * HEAD_DIM],
                preferred_element_type=f32,
            )
            for j in range(KV_HEADS)
        ],
        axis=0,
    )
    att_scr[...] = attended + fresh_prob * nv_scr[...]
    for copy in copies[6:]:
        copy.wait()
    squares = jnp.zeros((rows, HEAD_DIM), f32)
    for j in range(KV_HEADS):
        for g in range(GROUP):
            h = j * GROUP + g
            cols = slice(h * HEAD_DIM, (h + 1) * HEAD_DIM)
            at = slice(j * SLOT + g * rows, j * SLOT + (g + 1) * rows)
            piece = residual_ref[:, cols].astype(f32) + att_scr[at, :]
            stream_ref[:, cols] = piece
            squares = squares + piece * piece
    mean_square = jnp.sum(squares, axis=1, keepdims=True) * (1.0 / D)
    normed = stream_ref[...] * lax.rsqrt(mean_square + 1e-05) * gain_ref[...]
    first = lax.axis_index("sub") == 0
    low, high = normed[:, :half], normed[:, half:]
    lane = lax.broadcasted_iota(jnp.int32, (rows, LANES), 1)
    row = lax.broadcasted_iota(jnp.int32, (rows, LANES), 0)
    table = jnp.zeros((rows, LANES), f32)
    for r in range(rows):
        for c in range(2):
            here = jnp.logical_and(row == r, lane == ids_ref[c, r])
            table = jnp.where(here, levels_ref[c, r].astype(f32), table)
    own = jnp.concatenate([jnp.where(first, low, high), table], axis=1)
    other = jnp.concatenate([jnp.where(first, high, low), table], axis=1)
    for ref, value in ((own_ref, own), (other_ref, other)):
        ref[...] = jnp.concatenate(
            [jnp.where(first, value, 0.0), jnp.where(first, 0.0, value)], axis=0
        ).astype(jnp.bfloat16)
    for load in loads:
        load.wait()


def spread(scales, columns, dimension):
    blocks = scales.shape[dimension]
    block = lax.broadcasted_iota(jnp.int32, (blocks, columns), 0)
    column = lax.broadcasted_iota(jnp.int32, (blocks, columns), 1)
    pick = (column // QBLOCK == block).astype(jnp.float32)
    return lax.dot_general(
        scales,
        pick,
        (((dimension,), (0,)), ((), ())),
        precision=lax.Precision.HIGHEST,
        preferred_element_type=jnp.float32,
    )


def load_kernel(*refs, places, spreading):
    count = len(places)
    after_ref, scales = refs[0], refs[1 : 1 + 3 * spreading]
    refs = refs[1 + 3 * spreading :]
    sources, refs = refs[:count], refs[count:]
    refs[0][...] = after_ref[...]
    refs = refs[1:]
    rows_refs, refs = refs[: 3 * spreading], refs[3 * spreading :]
    targets, refs = refs[:count], refs[count:]
    load_sems = refs[0]
    loads = start_loads(places, sources, targets, load_sems)
    if spreading:
        held, sems = refs[1:4], refs[4]
        copies = [
            pltpu.make_async_copy(source, target, sems.at[i])
            for i, (source, target) in enumerate(zip(scales, held))
        ]
        for copy in copies:
            copy.start()
        for i, (copy, target, out_ref) in enumerate(zip(copies, held, rows_refs)):
            copy.wait()
            experts, _, columns = out_ref.shape
            for e in range(experts):
                out_ref[e] = spread(target[:, e, :], columns, 1 if i < 2 else 0)
    for load in loads:
        load.wait()


def scaled_product(left, pieces, scales_ref, expert, column, width):
    depth = pieces[0].shape[0] // QBLOCK
    total = None
    for k in range(len(pieces) * depth):
        at = (k % depth) * QBLOCK
        product = jnp.dot(
            left[:, k * QBLOCK : (k + 1) * QBLOCK],
            pieces[k // depth][at : at + QBLOCK, column : column + width],
            preferred_element_type=jnp.float32,
        )
        product = product * scales_ref[expert, k : k + 1, column : column + width]
        total = product if total is None else total + product
    return total


def gate_up_kernel(*refs, expert, places):
    count = len(places)
    x_ref, gate_s_ref, up_s_ref = refs[:3]
    gate, up = refs[3 : 3 + PIECES], refs[3 + PIECES : 3 + 2 * PIECES]
    refs = refs[3 + 2 * PIECES :]
    sources, out_ref, targets = refs[:count], refs[count], refs[count + 1 : 2 * count + 1]
    loads = start_loads(places, sources, targets, refs[-1])
    units = gate[0].shape[1]
    depth = gate[0].shape[0] * PIECES
    rows = x_ref.shape[0]
    block = min(rows, 64)
    width = min(units, WIDTH)
    for m in range(rows // block):
        at = slice(m * block, (m + 1) * block)
        left = x_ref[at, :depth]
        for column in range(0, units, width):
            out_ref[at, column : column + width] = scaled_product(
                left, gate, gate_s_ref, expert, column, width
            ).astype(jnp.bfloat16)
            out_ref[at, units + column : units + column + width] = scaled_product(
                left, up, up_s_ref, expert, column, width
            ).astype(jnp.bfloat16)
    for load in loads:
        load.wait()


def down_kernel(*refs, expert, experts, places):
    count = len(places)
    x_ref, mine, theirs, down_s_ref = refs[:4]
    down, refs = refs[4 : 4 + PIECES], refs[4 + PIECES :]
    before = None
    if expert > 0:
        before, refs = refs[0], refs[1:]
    sources, out_ref, targets = refs[:count], refs[count], refs[count + 1 : 2 * count + 1]
    loads = start_loads(places, sources, targets, refs[-1])
    columns = down[0].shape[1]
    units = down[0].shape[0] * PIECES
    rows, extended = x_ref.shape
    block = min(rows, 64)
    width = 256
    f32 = jnp.float32
    wanted = lax.axis_index("role") * experts + expert
    for m in range(rows // block):
        at = slice(m * block, (m + 1) * block)
        levels = x_ref[at, extended - LANES :].astype(f32)
        lane = lax.broadcasted_iota(jnp.int32, levels.shape, 1)
        level = jnp.sum(jnp.where(lane == wanted, levels, 0.0), axis=1, keepdims=True)
        share = level / jnp.sum(levels, axis=1, keepdims=True)
        chunks = []
        for u in range(0, units, width):
            gate = mine[at, u : u + width].astype(f32) + theirs[at, u : u + width].astype(f32)
            v = slice(units + u, units + u + width)
            up = mine[at, v].astype(f32) + theirs[at, v].astype(f32)
            silu = gate / (1.0 + jnp.exp(-gate))
            chunks.append((silu * up * share).astype(jnp.bfloat16))
        hidden = jnp.concatenate(chunks, axis=1)
        for column in range(0, columns, width):
            total = scaled_product(hidden, down, down_s_ref, expert, column, width)
            if before is not None:
                total = total + before[at, column : column + width]
            out_ref[at, column : column + width] = total.astype(out_ref.dtype)
    for load in loads:
        load.wait()


def finish_kernel(stream_ref, own_ref, other_ref, out_ref):
    half = D // 2
    rows = stream_ref.shape[0]
    first = lax.axis_index("sub") == 0
    own, other = (
        jnp.where(first, pair[:rows], pair[rows:])
        for pair in (own_ref[...].astype(jnp.float32), other_ref[...].astype(jnp.float32))
    )
    out_ref[:, :half] = (stream_ref[:, :half] + jnp.where(first, own, other)).astype(jnp.bfloat16)
    out_ref[:, half:] = (stream_ref[:, half:] + jnp.where(first, other, own)).astype(jnp.bfloat16)


def swap(x, axis, bit):
    count = lax.axis_size(axis)
    return lax.ppermute(x, axis, [(i, i ^ bit) for i in range(count)])


def bits(axis):
    return [1 << b for b in range(lax.axis_size(axis).bit_length() - 1)]


def add_bf16(a, b):
    return (a.astype(jnp.float32) + b.astype(jnp.float32)).astype(jnp.bfloat16)


def swap(x, axis, bit):
    count = lax.axis_size(axis)
    return lax.ppermute(x, axis, [(i, i ^ bit) for i in range(count)])


def bits(axis):
    return [1 << b for b in range(lax.axis_size(axis).bit_length() - 1)]


def add_bf16(a, b):
    return (a.astype(jnp.float32) + b.astype(jnp.float32)).astype(jnp.bfloat16)


class Loader:
    def __init__(self, gate, up, down):
        self.experts = gate.shape[0]
        self.arrays = {"gate": gate, "up": up, "down": down}
        self.waiting = [
            (name, e, piece)
            for names in (("gate", "up"), ("down",))
            for e in range(self.experts)
            for name in names
            for piece in range(PIECES)
        ]
        self.loaded = {}

    def take(self, count):
        taken, self.waiting = self.waiting[:count], self.waiting[count:]
        return taken

    def missing(self, expert, names):
        return sum(1 for name, e, _ in self.waiting if e == expert and name in names)

    def call(self, kernel, taken, inputs, specs, outputs, scratch, name, cost, **static):
        sources = [self.arrays[segment_name] for segment_name, _, _ in taken]
        shapes = [
            pltpu.VMEM((a.shape[1] // PIECES, a.shape[2]), a.dtype) for a in sources
        ]
        moved = sum(2 * math.prod(shape.shape) for shape in shapes)
        inputs = [
            pltpu.with_memory_space_constraint(x, pltpu.HBM) if spec is ANY else x
            for x, spec in zip(inputs, specs)
        ]
        sources = [pltpu.with_memory_space_constraint(x, pltpu.HBM) for x in sources]
        results = pl.pallas_call(
            functools.partial(kernel, places=tuple((e, p) for _, e, p in taken), **static),
            out_shape=tuple(outputs) + tuple(shapes),
            in_specs=list(specs) + [ANY] * len(taken),
            out_specs=tuple([VMEM] * (len(outputs) + len(taken))),
            scratch_shapes=list(scratch(len(taken))),
            compiler_params=pltpu.CompilerParams(vmem_limit_bytes=VMEM_LIMIT),
            cost_estimate=pl.CostEstimate(
                flops=0, bytes_accessed=cost + moved, transcendentals=0
            ),
            name=name,
        )(*inputs, *sources)
        for at, array in zip(taken, results[len(outputs) :]):
            self.loaded[at] = array
        return results[: len(outputs)]

    def pieces(self, name, expert):
        return [self.loaded[(name, expert, piece)] for piece in range(PIECES)]


def semaphores(count):
    return pltpu.SemaphoreType.DMA((max(count, 1),))


def load_more(loader, taken, after, scales):
    outputs, scratch = [jax.ShapeDtypeStruct(after.shape, after.dtype)], []
    if scales:
        experts, depth, units = loader.arrays["gate"].shape
        columns = loader.arrays["down"].shape[2]
        outputs += [
            jax.ShapeDtypeStruct((experts, depth // QBLOCK, units), jnp.float32),
            jax.ShapeDtypeStruct((experts, depth // QBLOCK, units), jnp.float32),
            jax.ShapeDtypeStruct((experts, units // QBLOCK, columns), jnp.float32),
        ]
        scratch = [pltpu.VMEM(s.shape, s.dtype) for s in scales] + [semaphores(3)]
    return loader.call(
        load_kernel,
        taken,
        [after, *scales],
        [VMEM] + [ANY] * len(scales),
        outputs,
        lambda count: [semaphores(count)] + scratch,
        "load",
        0,
        spreading=1 if scales else 0,
    )


def per_device(
    residual,
    query,
    new_key,
    new_value,
    cache_key,
    cache_value,
    lengths,
    norm_gain,
    expert_ids,
    gate_levels,
    gate_codes,
    gate_scales,
    up_codes,
    up_scales,
    down_codes,
    down_scales,
):
    rows = residual.shape[0]
    half = D // 2
    extended = half + LANES
    experts, _, units = gate_codes.shape
    loader = Loader(gate_codes, up_codes, down_codes)
    inputs = [
        query,
        new_key,
        new_value,
        lengths,
        cache_key,
        cache_value,
        residual,
        norm_gain.reshape(1, D),
        expert_ids.T,
        gate_levels.T,
    ]
    stacked = pltpu.VMEM((KV_HEADS * SLOT, HEAD_DIM), jnp.float32)
    held = [
        (pltpu.SMEM if x.dtype == jnp.int32 else pltpu.VMEM)(x.shape, x.dtype) for x in inputs
    ]
    own, other, stream = loader.call(
        attend_kernel,
        loader.take(LOAD_ATTEND),
        inputs,
        [ANY] * len(inputs),
        [
            jax.ShapeDtypeStruct((2 * rows, extended), jnp.bfloat16),
            jax.ShapeDtypeStruct((2 * rows, extended), jnp.bfloat16),
            jax.ShapeDtypeStruct((rows, D), jnp.float32),
        ],
        lambda count: held + [stacked] * 4 + [semaphores(len(inputs)), semaphores(count)],
        "attend",
        4 << 20,
    )
    scales = [
        gate_scales.transpose(1, 0, 2),
        up_scales.transpose(1, 0, 2),
        down_scales.transpose(2, 0, 1),
    ]
    gathered = own + swap(other, "sub", 1)
    steps = [("tp", bit) for bit in bits("tp")] + [("role", bit) for bit in bits("role")]
    spread_scales = None
    for number, (axis, bit) in enumerate(steps):
        arriving = swap(gathered, axis, bit)
        taken = loader.take(LOAD_STEP[min(number, len(LOAD_STEP) - 1)])
        if spread_scales is None:
            gathered, *spread_scales = load_more(loader, taken, gathered, scales)
        elif taken:
            (gathered,) = load_more(loader, taken, gathered, [])
        gathered = jnp.concatenate([gathered, arriving], axis=0)
    gate_s, up_s, down_s = spread_scales
    total_rows = gathered.shape[0]
    parts = []
    x = gathered
    for e in range(experts):
        missing = loader.missing(e, ("gate", "up"))
        if missing:
            (x,) = load_more(loader, loader.take(missing), x, [])
        (part,) = loader.call(
            gate_up_kernel,
            loader.take(LOAD_GATE_UP),
            [x, gate_s, up_s, *loader.pieces("gate", e), *loader.pieces("up", e)],
            [VMEM] * (3 + 2 * PIECES),
            [jax.ShapeDtypeStruct((total_rows, 2 * units), jnp.bfloat16)],
            lambda count: [semaphores(count)],
            "gate_up",
            8 << 20,
            expert=e,
        )
        parts.append((part, swap(part, "sub", 1)))
        x, _ = lax.optimization_barrier((x, part))
    carried = None
    for e in range(experts):
        last = e == experts - 1
        missing = loader.missing(e, ("down",))
        if missing:
            load_more(loader, loader.take(missing), parts[-1][0], [])
        before = [] if carried is None else [carried]
        (carried,) = loader.call(
            down_kernel,
            loader.take(LOAD_DOWN),
            [gathered, *parts[e], down_s, *loader.pieces("down", e), *before],
            [VMEM] * (4 + PIECES + len(before)),
            [
                jax.ShapeDtypeStruct(
                    (total_rows, half), jnp.bfloat16 if last else jnp.float32
                )
            ],
            lambda count: [semaphores(count)],
            "down",
            4 << 20,
            expert=e,
            experts=experts,
        )
    for axis, bit in reversed(steps):
        kept = carried.shape[0] // 2
        carried = add_bf16(carried[:kept], swap(carried[kept:], axis, bit))
    return pl.pallas_call(
        finish_kernel,
        out_shape=jax.ShapeDtypeStruct((rows, D), jnp.bfloat16),
        in_specs=[VMEM] * 3,
        out_specs=VMEM,
        compiler_params=pltpu.CompilerParams(vmem_limit_bytes=VMEM_LIMIT),
        name="finish",
    )(stream, carried, swap(carried, "sub", 1))


def solution(mesh):
    row = ("group", "role", "tp", "sub")
    in_specs = (
        P(row, None),
        P(row, None),
        P(row, None),
        P(row, None),
        P(row, None, None),
        P(row, None, None),
        P(row),
        P(),
        P(row, None),
        P(row, None),
        P("role", "sub", "tp"),
        P("role", "sub", "tp"),
        P("role", "sub", "tp"),
        P("role", "sub", "tp"),
        P("role", "tp", "sub"),
        P("role", "tp", "sub"),
    )
    return jax.shard_map(
        per_device, mesh=mesh, in_specs=in_specs, out_specs=P(row, None), check_vma=False
    )
```

```python
import functools
import math

import jax
import jax.numpy as jnp
from jax import lax
from jax.experimental import pallas as pl
from jax.experimental.pallas import tpu as pltpu
from jax.sharding import PartitionSpec as P

D = 3072
HEADS = 24
KV_HEADS = 8
HEAD_DIM = 128
EXPERTS = 4
QBLOCK = 128
LANES = 128
GROUP = HEADS // KV_HEADS
SLOT = 16
PIECES = 2
VMEM_LIMIT = 16 << 20

LOAD_ATTEND = 1
LOAD_STEP = (2, 1, 0)
LOAD_GATE_UP = 2
LOAD_DOWN = 1
WIDTH = 512

VMEM = pl.BlockSpec(memory_space=pltpu.VMEM)
ANY = pl.BlockSpec(memory_space=pltpu.HBM)


def segment(ref, expert, piece):
    depth = ref.shape[1] // PIECES
    return ref.at[expert, pl.ds(piece * depth, depth), :]


def start_loads(places, sources, targets, sems):
    copies = [
        pltpu.make_async_copy(segment(source, *place), target, sems.at[i])
        for i, (place, source, target) in enumerate(zip(places, sources, targets))
    ]
    for copy in copies:
        copy.start()
    return copies


def attend_kernel(*refs, places):
    count = len(places)
    inputs = refs[:10]
    sources = refs[10 : 10 + count]
    own_ref, other_ref, stream_ref = refs[10 + count : 13 + count]
    targets = refs[13 + count : 13 + 2 * count]
    scratch = refs[13 + 2 * count :]
    held = scratch[:10]
    q_scr, nk_scr, nv_scr, att_scr, in_sems, load_sems = scratch[10:]
    copies = [
        pltpu.make_async_copy(source, target, in_sems.at[i])
        for i, (source, target) in enumerate(zip(inputs, held))
    ]
    for copy in copies:
        copy.start()
    loads = start_loads(places, sources, targets, load_sems)
    (
        query_ref,
        new_key_ref,
        new_value_ref,
        lengths_ref,
        cache_key_ref,
        cache_value_ref,
        residual_ref,
        gain_ref,
        ids_ref,
        levels_ref,
    ) = held
    for copy in copies[:4]:
        copy.wait()
    rows, positions, _ = cache_key_ref.shape
    half = D // 2
    f32 = jnp.float32
    total = KV_HEADS * SLOT
    zeros = jnp.zeros((total, HEAD_DIM), f32)
    q_scr[...] = zeros
    nk_scr[...] = zeros
    nv_scr[...] = zeros
    for j in range(KV_HEADS):
        kv_cols = slice(j * HEAD_DIM, (j + 1) * HEAD_DIM)
        fresh_key = new_key_ref[:, kv_cols].astype(f32)
        fresh_value = new_value_ref[:, kv_cols].astype(f32)
        for g in range(GROUP):
            h = j * GROUP + g
            at = slice(j * SLOT + g * rows, j * SLOT + (g + 1) * rows)
            q_scr[at, :] = query_ref[:, h * HEAD_DIM : (h + 1) * HEAD_DIM].astype(f32)
            nk_scr[at, :] = fresh_key
            nv_scr[at, :] = fresh_value
    queries = q_scr[...]
    factor = 1.0 / math.sqrt(HEAD_DIM)
    fresh_score = jnp.sum(queries * nk_scr[...], axis=1, keepdims=True) * factor
    queries_bf = queries.astype(jnp.bfloat16)
    copies[4].wait()
    keys = cache_key_ref[...].reshape(rows * positions, KV_HEADS * HEAD_DIM)
    scores = jnp.concatenate(
        [
            lax.dot_general(
                queries_bf[j * SLOT : (j + 1) * SLOT],
                keys[:, j * HEAD_DIM : (j + 1) * HEAD_DIM],
                (((1,), (1,)), ((), ())),
                preferred_element_type=f32,
            )
            for j in range(KV_HEADS)
        ],
        axis=0,
    )
    row_of = lax.broadcasted_iota(jnp.int32, (total, positions), 0) % rows
    position = lax.broadcasted_iota(jnp.int32, (total, positions), 1)
    valid = [
        jnp.logical_and(row_of == r, position < lengths_ref[r]) for r in range(rows)
    ]
    pieces = [
        jnp.where(valid[r], scores[:, r * positions : (r + 1) * positions] * factor, -1e30)
        for r in range(rows)
    ]
    peak = functools.reduce(jnp.maximum, pieces)
    peak = jnp.maximum(jnp.max(peak, axis=1, keepdims=True), fresh_score)
    exps = [jnp.where(valid[r], jnp.exp(pieces[r] - peak), 0.0) for r in range(rows)]
    fresh_exp = jnp.exp(fresh_score - peak)
    denominator = jnp.sum(sum(exps[1:], exps[0]), axis=1, keepdims=True) + fresh_exp
    inverse = 1.0 / denominator
    probabilities = jnp.concatenate([(e * inverse).astype(jnp.bfloat16) for e in exps], axis=1)
    fresh_prob = (fresh_exp * inverse).astype(jnp.bfloat16).astype(f32)
    copies[5].wait()
    values = cache_value_ref[...].reshape(rows * positions, KV_HEADS * HEAD_DIM)
    attended = jnp.concatenate(
        [
            jnp.dot(
                probabilities[j * SLOT : (j + 1) * SLOT],
                values[:, j * HEAD_DIM : (j + 1) * HEAD_DIM],
                preferred_element_type=f32,
            )
            for j in range(KV_HEADS)
        ],
        axis=0,
    )
    att_scr[...] = attended + fresh_prob * nv_scr[...]
    for copy in copies[6:]:
        copy.wait()
    squares = jnp.zeros((rows, HEAD_DIM), f32)
    for j in range(KV_HEADS):
        for g in range(GROUP):
            h = j * GROUP + g
            cols = slice(h * HEAD_DIM, (h + 1) * HEAD_DIM)
            at = slice(j * SLOT + g * rows, j * SLOT + (g + 1) * rows)
            piece = residual_ref[:, cols].astype(f32) + att_scr[at, :]
            stream_ref[:, cols] = piece
            squares = squares + piece * piece
    mean_square = jnp.sum(squares, axis=1, keepdims=True) * (1.0 / D)
    normed = stream_ref[...] * lax.rsqrt(mean_square + 1e-05) * gain_ref[...]
    first = lax.axis_index("sub") == 0
    low, high = normed[:, :half], normed[:, half:]
    lane = lax.broadcasted_iota(jnp.int32, (rows, LANES), 1)
    row = lax.broadcasted_iota(jnp.int32, (rows, LANES), 0)
    table = jnp.zeros((rows, LANES), f32)
    for r in range(rows):
        for c in range(2):
            here = jnp.logical_and(row == r, lane == ids_ref[c, r])
            table = jnp.where(here, levels_ref[c, r].astype(f32), table)
    own = jnp.concatenate([jnp.where(first, low, high), table], axis=1)
    other = jnp.concatenate([jnp.where(first, high, low), table], axis=1)
    for ref, value in ((own_ref, own), (other_ref, other)):
        ref[...] = jnp.concatenate(
            [jnp.where(first, value, 0.0), jnp.where(first, 0.0, value)], axis=0
        ).astype(jnp.bfloat16)
    for load in loads:
        load.wait()


def spread(scales, columns, dimension):
    blocks = scales.shape[dimension]
    block = lax.broadcasted_iota(jnp.int32, (blocks, columns), 0)
    column = lax.broadcasted_iota(jnp.int32, (blocks, columns), 1)
    pick = (column // QBLOCK == block).astype(jnp.float32)
    return lax.dot_general(
        scales,
        pick,
        (((dimension,), (0,)), ((), ())),
        precision=lax.Precision.HIGHEST,
        preferred_element_type=jnp.float32,
    )


def load_kernel(*refs, places, spreading):
    count = len(places)
    after_ref, scales = refs[0], refs[1 : 1 + 3 * spreading]
    refs = refs[1 + 3 * spreading :]
    sources, refs = refs[:count], refs[count:]
    refs[0][...] = after_ref[...]
    refs = refs[1:]
    rows_refs, refs = refs[: 3 * spreading], refs[3 * spreading :]
    targets, refs = refs[:count], refs[count:]
    load_sems = refs[0]
    loads = start_loads(places, sources, targets, load_sems)
    if spreading:
        held, sems = refs[1:4], refs[4]
        copies = [
            pltpu.make_async_copy(source, target, sems.at[i])
            for i, (source, target) in enumerate(zip(scales, held))
        ]
        for copy in copies:
            copy.start()
        for i, (copy, target, out_ref) in enumerate(zip(copies, held, rows_refs)):
            copy.wait()
            experts, _, columns = out_ref.shape
            for e in range(experts):
                out_ref[e] = spread(target[:, e, :], columns, 1 if i < 2 else 0)
    for load in loads:
        load.wait()


def scaled_product(left, pieces, scales_ref, expert, column, width):
    depth = pieces[0].shape[0] // QBLOCK
    total = None
    for k in range(len(pieces) * depth):
        at = (k % depth) * QBLOCK
        product = jnp.dot(
            left[:, k * QBLOCK : (k + 1) * QBLOCK],
            pieces[k // depth][at : at + QBLOCK, column : column + width],
            preferred_element_type=jnp.float32,
        )
        product = product * scales_ref[expert, k : k + 1, column : column + width]
        total = product if total is None else total + product
    return total


def gate_up_kernel(*refs, expert, places):
    count = len(places)
    x_ref, gate_s_ref, up_s_ref = refs[:3]
    gate, up = refs[3 : 3 + PIECES], [refs[3 + PIECES].at[expert]]
    refs = refs[4 + PIECES :]
    sources, out_ref, targets = refs[:count], refs[count], refs[count + 1 : 2 * count + 1]
    loads = start_loads(places, sources, targets, refs[-1])
    units = gate[0].shape[1]
    depth = gate[0].shape[0] * PIECES
    rows = x_ref.shape[0]
    block = min(rows, 64)
    width = min(units, WIDTH)
    for m in range(rows // block):
        at = slice(m * block, (m + 1) * block)
        left = x_ref[at, :depth]
        for column in range(0, units, width):
            out_ref[at, column : column + width] = scaled_product(
                left, gate, gate_s_ref, expert, column, width
            ).astype(jnp.bfloat16)
            out_ref[at, units + column : units + column + width] = scaled_product(
                left, up, up_s_ref, expert, column, width
            ).astype(jnp.bfloat16)
    for load in loads:
        load.wait()


def down_kernel(*refs, expert, experts, places):
    count = len(places)
    x_ref, mine, theirs, down_s_ref = refs[:4]
    down, refs = [refs[4].at[expert]], refs[5:]
    before = None
    if expert > 0:
        before, refs = refs[0], refs[1:]
    sources, out_ref, targets = refs[:count], refs[count], refs[count + 1 : 2 * count + 1]
    loads = start_loads(places, sources, targets, refs[-1])
    columns = down[0].shape[1]
    units = down[0].shape[0]
    rows, extended = x_ref.shape
    block = min(rows, 64)
    width = 256
    f32 = jnp.float32
    wanted = lax.axis_index("role") * experts + expert
    for m in range(rows // block):
        at = slice(m * block, (m + 1) * block)
        levels = x_ref[at, extended - LANES :].astype(f32)
        lane = lax.broadcasted_iota(jnp.int32, levels.shape, 1)
        level = jnp.sum(jnp.where(lane == wanted, levels, 0.0), axis=1, keepdims=True)
        share = level / jnp.sum(levels, axis=1, keepdims=True)
        chunks = []
        for u in range(0, units, width):
            gate = mine[at, u : u + width].astype(f32) + theirs[at, u : u + width].astype(f32)
            v = slice(units + u, units + u + width)
            up = mine[at, v].astype(f32) + theirs[at, v].astype(f32)
            silu = gate / (1.0 + jnp.exp(-gate))
            chunks.append((silu * up * share).astype(jnp.bfloat16))
        hidden = jnp.concatenate(chunks, axis=1)
        for column in range(0, columns, width):
            total = scaled_product(hidden, down, down_s_ref, expert, column, width)
            if before is not None:
                total = total + before[at, column : column + width]
            out_ref[at, column : column + width] = total.astype(out_ref.dtype)
    for load in loads:
        load.wait()


def finish_kernel(stream_ref, own_ref, other_ref, out_ref):
    half = D // 2
    rows = stream_ref.shape[0]
    first = lax.axis_index("sub") == 0
    own, other = (
        jnp.where(first, pair[:rows], pair[rows:])
        for pair in (own_ref[...].astype(jnp.float32), other_ref[...].astype(jnp.float32))
    )
    out_ref[:, :half] = (stream_ref[:, :half] + jnp.where(first, own, other)).astype(jnp.bfloat16)
    out_ref[:, half:] = (stream_ref[:, half:] + jnp.where(first, other, own)).astype(jnp.bfloat16)


def swap(x, axis, bit):
    count = lax.axis_size(axis)
    return lax.ppermute(x, axis, [(i, i ^ bit) for i in range(count)])


def bits(axis):
    return [1 << b for b in range(lax.axis_size(axis).bit_length() - 1)]


def add_bf16(a, b):
    return (a.astype(jnp.float32) + b.astype(jnp.float32)).astype(jnp.bfloat16)


def swap(x, axis, bit):
    count = lax.axis_size(axis)
    return lax.ppermute(x, axis, [(i, i ^ bit) for i in range(count)])


def bits(axis):
    return [1 << b for b in range(lax.axis_size(axis).bit_length() - 1)]


def add_bf16(a, b):
    return (a.astype(jnp.float32) + b.astype(jnp.float32)).astype(jnp.bfloat16)


class Loader:
    def __init__(self, gate, up, down):
        self.experts = gate.shape[0]
        self.arrays = {"gate": gate, "up": up, "down": down}
        self.waiting = [
            (name, e, piece)
            for names in (("gate",),)
            for e in range(self.experts)
            for name in names
            for piece in range(PIECES)
        ]
        self.loaded = {}

    def take(self, count):
        taken, self.waiting = self.waiting[:count], self.waiting[count:]
        return taken

    def missing(self, expert, names):
        return sum(1 for name, e, _ in self.waiting if e == expert and name in names)

    def call(self, kernel, taken, inputs, specs, outputs, scratch, name, cost, **static):
        sources = [self.arrays[segment_name] for segment_name, _, _ in taken]
        shapes = [
            pltpu.VMEM((a.shape[1] // PIECES, a.shape[2]), a.dtype) for a in sources
        ]
        moved = sum(2 * math.prod(shape.shape) for shape in shapes)
        inputs = [
            pltpu.with_memory_space_constraint(x, pltpu.HBM) if spec is ANY else x
            for x, spec in zip(inputs, specs)
        ]
        sources = [pltpu.with_memory_space_constraint(x, pltpu.HBM) for x in sources]
        results = pl.pallas_call(
            functools.partial(kernel, places=tuple((e, p) for _, e, p in taken), **static),
            out_shape=tuple(outputs) + tuple(shapes),
            in_specs=list(specs) + [ANY] * len(taken),
            out_specs=tuple([VMEM] * (len(outputs) + len(taken))),
            scratch_shapes=list(scratch(len(taken))),
            compiler_params=pltpu.CompilerParams(vmem_limit_bytes=VMEM_LIMIT),
            cost_estimate=pl.CostEstimate(
                flops=0, bytes_accessed=cost + moved, transcendentals=0
            ),
            name=name,
        )(*inputs, *sources)
        for at, array in zip(taken, results[len(outputs) :]):
            self.loaded[at] = array
        return results[: len(outputs)]

    def pieces(self, name, expert):
        return [self.loaded[(name, expert, piece)] for piece in range(PIECES)]


def semaphores(count):
    return pltpu.SemaphoreType.DMA((max(count, 1),))


def load_more(loader, taken, after, scales):
    outputs, scratch = [jax.ShapeDtypeStruct(after.shape, after.dtype)], []
    if scales:
        experts, depth, units = loader.arrays["gate"].shape
        columns = loader.arrays["down"].shape[2]
        outputs += [
            jax.ShapeDtypeStruct((experts, depth // QBLOCK, units), jnp.float32),
            jax.ShapeDtypeStruct((experts, depth // QBLOCK, units), jnp.float32),
            jax.ShapeDtypeStruct((experts, units // QBLOCK, columns), jnp.float32),
        ]
        scratch = [pltpu.VMEM(s.shape, s.dtype) for s in scales] + [semaphores(3)]
    return loader.call(
        load_kernel,
        taken,
        [after, *scales],
        [VMEM] + [ANY] * len(scales),
        outputs,
        lambda count: [semaphores(count)] + scratch,
        "load",
        1 << 20,
        spreading=1 if scales else 0,
    )


def per_device(
    residual,
    query,
    new_key,
    new_value,
    cache_key,
    cache_value,
    lengths,
    norm_gain,
    expert_ids,
    gate_levels,
    gate_codes,
    gate_scales,
    up_codes,
    up_scales,
    down_codes,
    down_scales,
):
    rows = residual.shape[0]
    half = D // 2
    extended = half + LANES
    experts, _, units = gate_codes.shape
    loader = Loader(gate_codes, up_codes, down_codes)
    inputs = [
        query,
        new_key,
        new_value,
        lengths,
        cache_key,
        cache_value,
        residual,
        norm_gain.reshape(1, D),
        expert_ids.T,
        gate_levels.T,
    ]
    stacked = pltpu.VMEM((KV_HEADS * SLOT, HEAD_DIM), jnp.float32)
    held = [
        (pltpu.SMEM if x.dtype == jnp.int32 else pltpu.VMEM)(x.shape, x.dtype) for x in inputs
    ]
    own, other, stream = loader.call(
        attend_kernel,
        loader.take(LOAD_ATTEND),
        inputs,
        [ANY] * len(inputs),
        [
            jax.ShapeDtypeStruct((2 * rows, extended), jnp.bfloat16),
            jax.ShapeDtypeStruct((2 * rows, extended), jnp.bfloat16),
            jax.ShapeDtypeStruct((rows, D), jnp.float32),
        ],
        lambda count: held + [stacked] * 4 + [semaphores(len(inputs)), semaphores(count)],
        "attend",
        4 << 20,
    )
    scales = [
        gate_scales.transpose(1, 0, 2),
        up_scales.transpose(1, 0, 2),
        down_scales.transpose(2, 0, 1),
    ]
    gathered = own + swap(other, "sub", 1)
    steps = [("tp", bit) for bit in bits("tp")] + [("role", bit) for bit in bits("role")]
    spread_scales = None
    for number, (axis, bit) in enumerate(steps):
        arriving = swap(gathered, axis, bit)
        taken = loader.take(LOAD_STEP[min(number, len(LOAD_STEP) - 1)])
        if spread_scales is None:
            gathered, *spread_scales = load_more(loader, taken, gathered, scales)
        elif taken:
            (gathered,) = load_more(loader, taken, gathered, [])
        gathered = jnp.concatenate([gathered, arriving], axis=0)
    gate_s, up_s, down_s = spread_scales
    total_rows = gathered.shape[0]
    parts = []
    x = gathered
    for e in range(experts):
        missing = loader.missing(e, ("gate", "up"))
        if missing:
            (x,) = load_more(loader, loader.take(missing), x, [])
        (part,) = loader.call(
            gate_up_kernel,
            loader.take(LOAD_GATE_UP),
            [x, gate_s, up_s, *loader.pieces("gate", e), up_codes],
            [VMEM] * (4 + PIECES),
            [jax.ShapeDtypeStruct((total_rows, 2 * units), jnp.bfloat16)],
            lambda count: [semaphores(count)],
            "gate_up",
            2 << 20,
            expert=e,
        )
        parts.append((part, swap(part, "sub", 1)))
        x, _ = lax.optimization_barrier((x, part))
    carried = None
    for e in range(experts):
        last = e == experts - 1
        before = [] if carried is None else [carried]
        (carried,) = loader.call(
            down_kernel,
            loader.take(LOAD_DOWN),
            [gathered, *parts[e], down_s, down_codes, *before],
            [VMEM] * (5 + len(before)),
            [
                jax.ShapeDtypeStruct(
                    (total_rows, half), jnp.bfloat16 if last else jnp.float32
                )
            ],
            lambda count: [semaphores(count)],
            "down",
            4 << 20,
            expert=e,
            experts=experts,
        )
    for axis, bit in reversed(steps):
        kept = carried.shape[0] // 2
        carried = add_bf16(carried[:kept], swap(carried[kept:], axis, bit))
    return pl.pallas_call(
        finish_kernel,
        out_shape=jax.ShapeDtypeStruct((rows, D), jnp.bfloat16),
        in_specs=[VMEM] * 3,
        out_specs=VMEM,
        compiler_params=pltpu.CompilerParams(vmem_limit_bytes=VMEM_LIMIT),
        name="finish",
    )(stream, carried, swap(carried, "sub", 1))


def solution(mesh):
    row = ("group", "role", "tp", "sub")
    in_specs = (
        P(row, None),
        P(row, None),
        P(row, None),
        P(row, None),
        P(row, None, None),
        P(row, None, None),
        P(row),
        P(),
        P(row, None),
        P(row, None),
        P("role", "sub", "tp"),
        P("role", "sub", "tp"),
        P("role", "sub", "tp"),
        P("role", "sub", "tp"),
        P("role", "tp", "sub"),
        P("role", "tp", "sub"),
    )
    return jax.shard_map(
        per_device, mesh=mesh, in_specs=in_specs, out_specs=P(row, None), check_vma=False
    )
```

```python
import functools
import math

import jax
import jax.numpy as jnp
from jax import lax
from jax.experimental import pallas as pl
from jax.experimental.pallas import tpu as pltpu
from jax.sharding import PartitionSpec as P

D = 3072
HEADS = 24
KV_HEADS = 8
HEAD_DIM = 128
EXPERTS = 4
QBLOCK = 128
LANES = 128
GROUP = HEADS // KV_HEADS
SLOT = 16
PIECES = 2
VMEM_LIMIT = 16 << 20

LOAD_ATTEND = 1
LOAD_STEP = (1, 1, 1)
LOAD_GATE_UP = 2
LOAD_DOWN = 1
WIDTH = 512

VMEM = pl.BlockSpec(memory_space=pltpu.VMEM)
ANY = pl.BlockSpec(memory_space=pltpu.HBM)


def segment(ref, expert, piece):
    depth = ref.shape[1] // PIECES
    return ref.at[expert, pl.ds(piece * depth, depth), :]


def start_loads(places, sources, targets, sems):
    copies = [
        pltpu.make_async_copy(segment(source, *place), target, sems.at[i])
        for i, (place, source, target) in enumerate(zip(places, sources, targets))
    ]
    for copy in copies:
        copy.start()
    return copies


def attend_kernel(*refs, places):
    count = len(places)
    inputs = refs[:10]
    sources = refs[10 : 10 + count]
    x_ref, stream_ref = refs[10 + count : 12 + count]
    targets = refs[12 + count : 12 + 2 * count]
    scratch = refs[12 + 2 * count :]
    held = scratch[:10]
    q_scr, nk_scr, nv_scr, att_scr, in_sems, load_sems = scratch[10:]
    copies = [
        pltpu.make_async_copy(source, target, in_sems.at[i])
        for i, (source, target) in enumerate(zip(inputs, held))
    ]
    for copy in copies:
        copy.start()
    loads = start_loads(places, sources, targets, load_sems)
    (
        query_ref,
        new_key_ref,
        new_value_ref,
        lengths_ref,
        cache_key_ref,
        cache_value_ref,
        residual_ref,
        gain_ref,
        ids_ref,
        levels_ref,
    ) = held
    for copy in copies[:4]:
        copy.wait()
    rows, positions, _ = cache_key_ref.shape
    f32 = jnp.float32
    total = KV_HEADS * SLOT
    zeros = jnp.zeros((total, HEAD_DIM), f32)
    q_scr[...] = zeros
    nk_scr[...] = zeros
    nv_scr[...] = zeros
    for j in range(KV_HEADS):
        kv_cols = slice(j * HEAD_DIM, (j + 1) * HEAD_DIM)
        fresh_key = new_key_ref[:, kv_cols].astype(f32)
        fresh_value = new_value_ref[:, kv_cols].astype(f32)
        for g in range(GROUP):
            h = j * GROUP + g
            at = slice(j * SLOT + g * rows, j * SLOT + (g + 1) * rows)
            q_scr[at, :] = query_ref[:, h * HEAD_DIM : (h + 1) * HEAD_DIM].astype(f32)
            nk_scr[at, :] = fresh_key
            nv_scr[at, :] = fresh_value
    queries = q_scr[...]
    factor = 1.0 / math.sqrt(HEAD_DIM)
    fresh_score = jnp.sum(queries * nk_scr[...], axis=1, keepdims=True) * factor
    queries_bf = queries.astype(jnp.bfloat16)
    copies[4].wait()
    keys = cache_key_ref[...].reshape(rows * positions, KV_HEADS * HEAD_DIM)
    scores = jnp.concatenate(
        [
            lax.dot_general(
                queries_bf[j * SLOT : (j + 1) * SLOT],
                keys[:, j * HEAD_DIM : (j + 1) * HEAD_DIM],
                (((1,), (1,)), ((), ())),
                preferred_element_type=f32,
            )
            for j in range(KV_HEADS)
        ],
        axis=0,
    )
    row_of = lax.broadcasted_iota(jnp.int32, (total, positions), 0) % rows
    position = lax.broadcasted_iota(jnp.int32, (total, positions), 1)
    valid = [
        jnp.logical_and(row_of == r, position < lengths_ref[r]) for r in range(rows)
    ]
    pieces = [
        jnp.where(valid[r], scores[:, r * positions : (r + 1) * positions] * factor, -1e30)
        for r in range(rows)
    ]
    peak = functools.reduce(jnp.maximum, pieces)
    peak = jnp.maximum(jnp.max(peak, axis=1, keepdims=True), fresh_score)
    exps = [jnp.where(valid[r], jnp.exp(pieces[r] - peak), 0.0) for r in range(rows)]
    fresh_exp = jnp.exp(fresh_score - peak)
    denominator = jnp.sum(sum(exps[1:], exps[0]), axis=1, keepdims=True) + fresh_exp
    inverse = 1.0 / denominator
    probabilities = jnp.concatenate([(e * inverse).astype(jnp.bfloat16) for e in exps], axis=1)
    fresh_prob = (fresh_exp * inverse).astype(jnp.bfloat16).astype(f32)
    copies[5].wait()
    values = cache_value_ref[...].reshape(rows * positions, KV_HEADS * HEAD_DIM)
    attended = jnp.concatenate(
        [
            jnp.dot(
                probabilities[j * SLOT : (j + 1) * SLOT],
                values[:, j * HEAD_DIM : (j + 1) * HEAD_DIM],
                preferred_element_type=f32,
            )
            for j in range(KV_HEADS)
        ],
        axis=0,
    )
    att_scr[...] = attended + fresh_prob * nv_scr[...]
    for copy in copies[6:]:
        copy.wait()
    squares = jnp.zeros((rows, HEAD_DIM), f32)
    for j in range(KV_HEADS):
        for g in range(GROUP):
            h = j * GROUP + g
            cols = slice(h * HEAD_DIM, (h + 1) * HEAD_DIM)
            at = slice(j * SLOT + g * rows, j * SLOT + (g + 1) * rows)
            piece = residual_ref[:, cols].astype(f32) + att_scr[at, :]
            stream_ref[:, cols] = piece
            squares = squares + piece * piece
    mean_square = jnp.sum(squares, axis=1, keepdims=True) * (1.0 / D)
    normed = stream_ref[...] * lax.rsqrt(mean_square + 1e-05) * gain_ref[...]
    lane = lax.broadcasted_iota(jnp.int32, (rows, LANES), 1)
    row = lax.broadcasted_iota(jnp.int32, (rows, LANES), 0)
    table = jnp.zeros((rows, LANES), f32)
    for r in range(rows):
        for c in range(2):
            here = jnp.logical_and(row == r, lane == ids_ref[c, r])
            table = jnp.where(here, levels_ref[c, r].astype(f32), table)
    x_ref[...] = jnp.concatenate([normed, table], axis=1).astype(jnp.bfloat16)
    for load in loads:
        load.wait()


def spread(scales, columns, dimension):
    blocks = scales.shape[dimension]
    block = lax.broadcasted_iota(jnp.int32, (blocks, columns), 0)
    column = lax.broadcasted_iota(jnp.int32, (blocks, columns), 1)
    pick = (column // QBLOCK == block).astype(jnp.float32)
    return lax.dot_general(
        scales,
        pick,
        (((dimension,), (0,)), ((), ())),
        precision=lax.Precision.HIGHEST,
        preferred_element_type=jnp.float32,
    )


def load_kernel(*refs, places, spreading):
    count = len(places)
    after_ref, scales = refs[0], refs[1 : 1 + 3 * spreading]
    refs = refs[1 + 3 * spreading :]
    sources, refs = refs[:count], refs[count:]
    refs[0][...] = after_ref[...]
    refs = refs[1:]
    rows_refs, refs = refs[: 3 * spreading], refs[3 * spreading :]
    targets, refs = refs[:count], refs[count:]
    load_sems = refs[0]
    loads = start_loads(places, sources, targets, load_sems)
    if spreading:
        held, sems = refs[1:4], refs[4]
        copies = [
            pltpu.make_async_copy(source, target, sems.at[i])
            for i, (source, target) in enumerate(zip(scales, held))
        ]
        for copy in copies:
            copy.start()
        for i, (copy, target, out_ref) in enumerate(zip(copies, held, rows_refs)):
            copy.wait()
            experts, _, columns = out_ref.shape
            for e in range(experts):
                out_ref[e] = spread(target[:, e, :], columns, 1 if i < 2 else 0)
    for load in loads:
        load.wait()


def scaled_product(left, pieces, scales_ref, expert, column, width):
    depth = pieces[0].shape[0] // QBLOCK
    total = None
    for k in range(len(pieces) * depth):
        at = (k % depth) * QBLOCK
        product = jnp.dot(
            left[:, k * QBLOCK : (k + 1) * QBLOCK],
            pieces[k // depth][at : at + QBLOCK, column : column + width],
            preferred_element_type=jnp.float32,
        )
        product = product * scales_ref[expert, k : k + 1, column : column + width]
        total = product if total is None else total + product
    return total


def split_kernel(near_ref, far_ref, kept_ref, sent_ref):
    half = D // 2
    first = lax.axis_index("sub") == 0
    count = near_ref.shape[0]
    for i, ref in enumerate((near_ref, far_ref)):
        at = slice(i * count, (i + 1) * count)
        low, high, table = ref[:, :half], ref[:, half:D], ref[:, D:]
        kept_ref[at, :half] = jnp.where(first, low, high)
        sent_ref[at, :half] = jnp.where(first, high, low)
        kept_ref[at, half:] = table
        sent_ref[at, half:] = table


def chip_rows(kept_ref, other_ref, start, block, columns):
    first = lax.axis_index("sub") == 0
    count = kept_ref.shape[0]
    parts = []
    while block > 0:
        core, row = start // count, start % count
        size = min(block, count - row)
        at = slice(row, row + size)
        pair = kept_ref[at, columns], other_ref[at, columns]
        parts.append(jnp.where(first, pair[core], pair[1 - core]))
        start, block = start + size, block - size
    return parts[0] if len(parts) == 1 else jnp.concatenate(parts, axis=0)


def gate_up_kernel(*refs, expert, places):
    count = len(places)
    kept_ref, other_ref, gate_s_ref, up_s_ref = refs[:4]
    gate, up = refs[4 : 4 + PIECES], [refs[4 + PIECES].at[expert]]
    refs = refs[5 + PIECES :]
    sources, out_ref, targets = refs[:count], refs[count], refs[count + 1 : 2 * count + 1]
    loads = start_loads(places, sources, targets, refs[-1])
    units = gate[0].shape[1]
    depth = gate[0].shape[0] * PIECES
    rows = 2 * kept_ref.shape[0]
    block = min(rows, 64)
    width = min(units, WIDTH)
    for m in range(rows // block):
        at = slice(m * block, (m + 1) * block)
        left = chip_rows(kept_ref, other_ref, m * block, block, slice(0, depth))
        for column in range(0, units, width):
            out_ref[at, column : column + width] = scaled_product(
                left, gate, gate_s_ref, expert, column, width
            ).astype(jnp.bfloat16)
            out_ref[at, units + column : units + column + width] = scaled_product(
                left, up, up_s_ref, expert, column, width
            ).astype(jnp.bfloat16)
    for load in loads:
        load.wait()


def down_kernel(*refs, expert, experts, places):
    count = len(places)
    last = expert == experts - 1
    kept_ref, other_ref, mine, theirs, down_s_ref = refs[:5]
    down, refs = [refs[5].at[expert]], refs[6:]
    before = None
    if expert > 0:
        before, refs = refs[0], refs[1:]
    sources, refs = refs[:count], refs[count:]
    outputs, refs = refs[: 1 + last], refs[1 + last :]
    loads = start_loads(places, sources, refs[:count], refs[count])
    out_ref = refs[count + 1] if last else outputs[0]
    columns = down[0].shape[1]
    units = down[0].shape[0]
    rows, extended = 2 * kept_ref.shape[0], kept_ref.shape[1]
    block = min(rows, 64)
    width = 256
    f32 = jnp.float32
    wanted = lax.axis_index("role") * experts + expert
    for m in range(rows // block):
        at = slice(m * block, (m + 1) * block)
        levels = chip_rows(
            kept_ref, other_ref, m * block, block, slice(extended - LANES, extended)
        ).astype(f32)
        lane = lax.broadcasted_iota(jnp.int32, levels.shape, 1)
        level = jnp.sum(jnp.where(lane == wanted, levels, 0.0), axis=1, keepdims=True)
        share = level / jnp.sum(levels, axis=1, keepdims=True)
        chunks = []
        for u in range(0, units, width):
            gate = mine[at, u : u + width].astype(f32) + theirs[at, u : u + width].astype(f32)
            v = slice(units + u, units + u + width)
            up = mine[at, v].astype(f32) + theirs[at, v].astype(f32)
            silu = gate / (1.0 + jnp.exp(-gate))
            chunks.append((silu * up * share).astype(jnp.bfloat16))
        hidden = jnp.concatenate(chunks, axis=1)
        for column in range(0, columns, width):
            total = scaled_product(hidden, down, down_s_ref, expert, column, width)
            if before is not None:
                total = total + before[at, column : column + width]
            out_ref[at, column : column + width] = total
    if last:
        first = lax.axis_index("sub") == 0
        low, high = out_ref[: rows // 2, :], out_ref[rows // 2 :, :]
        outputs[0][...] = jnp.where(first, low, high).astype(jnp.bfloat16)
        outputs[1][...] = jnp.where(first, high, low).astype(jnp.bfloat16)
    for load in loads:
        load.wait()


def join_kernel(kept_ref, other_ref, near_ref, far_ref):
    half = D // 2
    first = lax.axis_index("sub") == 0
    count = near_ref.shape[0]
    for ref, at in ((near_ref, slice(0, count)), (far_ref, slice(count, 2 * count))):
        kept, other = kept_ref[at, :], other_ref[at, :]
        ref[:, :half] = jnp.where(first, kept, other)
        ref[:, half:] = jnp.where(first, other, kept)


def finish_kernel(stream_ref, kept_ref, other_ref, out_ref):
    f32 = jnp.float32
    total = stream_ref[...] + (kept_ref[...].astype(f32) + other_ref[...].astype(f32))
    out_ref[...] = total.astype(jnp.bfloat16)


def swap(x, axis, bit):
    if axis is None:
        return lax.ppermute(x, "sub", [(0, 1), (1, 0)])
    count = 2 * lax.axis_size(axis)
    return lax.ppermute(x, (axis, "sub"), [(i, i ^ (2 * bit + 1)) for i in range(count)])


def bits(axis):
    return [1 << b for b in reversed(range(lax.axis_size(axis).bit_length() - 1))]


def local_call(kernel, outputs, inputs, name):
    return pl.pallas_call(
        kernel,
        out_shape=outputs,
        in_specs=[VMEM] * len(inputs),
        out_specs=jax.tree.map(lambda _: VMEM, outputs),
        compiler_params=pltpu.CompilerParams(vmem_limit_bytes=VMEM_LIMIT),
        name=name,
    )(*inputs)


def add_bf16(a, b):
    return (a.astype(jnp.float32) + b.astype(jnp.float32)).astype(jnp.bfloat16)


class Loader:
    def __init__(self, gate, up, down):
        self.experts = gate.shape[0]
        self.arrays = {"gate": gate, "up": up, "down": down}
        self.waiting = [
            (name, e, piece)
            for names in (("gate",),)
            for e in range(self.experts)
            for name in names
            for piece in range(PIECES)
        ]
        self.loaded = {}

    def take(self, count):
        taken, self.waiting = self.waiting[:count], self.waiting[count:]
        return taken

    def missing(self, expert, names):
        return sum(1 for name, e, _ in self.waiting if e == expert and name in names)

    def call(self, kernel, taken, inputs, specs, outputs, scratch, name, cost, **static):
        sources = [self.arrays[segment_name] for segment_name, _, _ in taken]
        shapes = [
            pltpu.VMEM((a.shape[1] // PIECES, a.shape[2]), a.dtype) for a in sources
        ]
        moved = sum(2 * math.prod(shape.shape) for shape in shapes)
        inputs = [
            pltpu.with_memory_space_constraint(x, pltpu.HBM) if spec is ANY else x
            for x, spec in zip(inputs, specs)
        ]
        sources = [pltpu.with_memory_space_constraint(x, pltpu.HBM) for x in sources]
        results = pl.pallas_call(
            functools.partial(kernel, places=tuple((e, p) for _, e, p in taken), **static),
            out_shape=tuple(outputs) + tuple(shapes),
            in_specs=list(specs) + [ANY] * len(taken),
            out_specs=tuple([VMEM] * (len(outputs) + len(taken))),
            scratch_shapes=list(scratch(len(taken))),
            compiler_params=pltpu.CompilerParams(vmem_limit_bytes=VMEM_LIMIT),
            cost_estimate=pl.CostEstimate(
                flops=0, bytes_accessed=cost + moved, transcendentals=0
            ),
            name=name,
        )(*inputs, *sources)
        for at, array in zip(taken, results[len(outputs) :]):
            self.loaded[at] = array
        return results[: len(outputs)]

    def pieces(self, name, expert):
        return [self.loaded[(name, expert, piece)] for piece in range(PIECES)]


def semaphores(count):
    return pltpu.SemaphoreType.DMA((max(count, 1),))


def load_more(loader, taken, after, scales):
    outputs, scratch = [jax.ShapeDtypeStruct(after.shape, after.dtype)], []
    if scales:
        experts, depth, units = loader.arrays["gate"].shape
        columns = loader.arrays["down"].shape[2]
        outputs += [
            jax.ShapeDtypeStruct((experts, depth // QBLOCK, units), jnp.float32),
            jax.ShapeDtypeStruct((experts, depth // QBLOCK, units), jnp.float32),
            jax.ShapeDtypeStruct((experts, units // QBLOCK, columns), jnp.float32),
        ]
        scratch = [pltpu.VMEM(s.shape, s.dtype) for s in scales] + [semaphores(3)]
    return loader.call(
        load_kernel,
        taken,
        [after, *scales],
        [VMEM] + [ANY] * len(scales),
        outputs,
        lambda count: [semaphores(count)] + scratch,
        "load",
        1 << 20,
        spreading=1 if scales else 0,
    )


def per_device(
    residual,
    query,
    new_key,
    new_value,
    cache_key,
    cache_value,
    lengths,
    norm_gain,
    expert_ids,
    gate_levels,
    gate_codes,
    gate_scales,
    up_codes,
    up_scales,
    down_codes,
    down_scales,
):
    rows = residual.shape[0]
    half = D // 2
    extended = half + LANES
    experts, _, units = gate_codes.shape
    loader = Loader(gate_codes, up_codes, down_codes)
    inputs = [
        query,
        new_key,
        new_value,
        lengths,
        cache_key,
        cache_value,
        residual,
        norm_gain.reshape(1, D),
        expert_ids.T,
        gate_levels.T,
    ]
    stacked = pltpu.VMEM((KV_HEADS * SLOT, HEAD_DIM), jnp.float32)
    held = [
        (pltpu.SMEM if x.dtype == jnp.int32 else pltpu.VMEM)(x.shape, x.dtype) for x in inputs
    ]
    x, stream = loader.call(
        attend_kernel,
        loader.take(LOAD_ATTEND),
        inputs,
        [ANY] * len(inputs),
        [
            jax.ShapeDtypeStruct((rows, D + LANES), jnp.bfloat16),
            jax.ShapeDtypeStruct((rows, D), jnp.float32),
        ],
        lambda count: held + [stacked] * 4 + [semaphores(len(inputs)), semaphores(count)],
        "attend",
        4 << 20,
    )
    scales = [
        gate_scales.transpose(1, 0, 2),
        up_scales.transpose(1, 0, 2),
        down_scales.transpose(2, 0, 1),
    ]
    steps = [("tp", bit) for bit in bits("tp")] + [("role", bit) for bit in bits("role")]
    spread_scales = None
    near, far = x, None
    for number, (axis, bit) in enumerate(steps):
        if far is not None:
            near = jnp.concatenate([near, far], axis=0)
        far = swap(near, axis, bit)
        taken = loader.take(LOAD_STEP[min(number, len(LOAD_STEP) - 1)])
        if spread_scales is None:
            near, *spread_scales = load_more(loader, taken, near, scales)
        elif taken:
            (near,) = load_more(loader, taken, near, [])
    gate_s, up_s, down_s = spread_scales
    count = 2 * near.shape[0]
    piece = jax.ShapeDtypeStruct((count, extended), jnp.bfloat16)
    kept, sent = local_call(split_kernel, (piece, piece), (near, far), "split")
    other = swap(sent, None, 0)
    parts = []
    before = other
    for e in range(experts):
        missing = loader.missing(e, ("gate",))
        if missing:
            (before,) = load_more(loader, loader.take(missing), before, [])
        (part,) = loader.call(
            gate_up_kernel,
            loader.take(LOAD_GATE_UP),
            [kept, before, gate_s, up_s, *loader.pieces("gate", e), up_codes],
            [VMEM] * (5 + PIECES),
            [jax.ShapeDtypeStruct((2 * count, 2 * units), jnp.bfloat16)],
            lambda loads: [semaphores(loads)],
            "gate_up",
            2 << 20,
            expert=e,
        )
        parts.append((part, swap(part, None, 0)))
        before, _ = lax.optimization_barrier((before, part))
    carried = []
    for e in range(experts):
        last = e == experts - 1
        sums = jax.ShapeDtypeStruct((2 * count, half), jnp.float32)
        returned = jax.ShapeDtypeStruct((count, half), jnp.bfloat16)
        carried = loader.call(
            down_kernel,
            loader.take(LOAD_DOWN),
            [kept, other, *parts[e], down_s, down_codes, *carried],
            [VMEM] * (6 + len(carried)),
            [returned, returned] if last else [sums],
            lambda loads: [semaphores(loads)] + ([pltpu.VMEM(sums.shape, sums.dtype)] if last else []),
            "down",
            4 << 20,
            expert=e,
            experts=experts,
        )
    kept, sent = carried
    piece = jax.ShapeDtypeStruct((count // 2, D), jnp.bfloat16)
    near, far = local_call(join_kernel, (piece, piece), (kept, swap(sent, None, 0)), "join")
    for axis, bit in reversed(steps[1:]):
        carried = add_bf16(near, swap(far, axis, bit))
        middle = carried.shape[0] // 2
        near, far = carried[:middle], carried[middle:]
    out = jax.ShapeDtypeStruct((rows, D), jnp.bfloat16)
    return local_call(finish_kernel, out, (stream, near, swap(far, *steps[0])), "finish")


def solution(mesh):
    row = ("group", "role", "tp", "sub")
    in_specs = (
        P(row, None),
        P(row, None),
        P(row, None),
        P(row, None),
        P(row, None, None),
        P(row, None, None),
        P(row),
        P(),
        P(row, None),
        P(row, None),
        P("role", "sub", "tp"),
        P("role", "sub", "tp"),
        P("role", "sub", "tp"),
        P("role", "sub", "tp"),
        P("role", "tp", "sub"),
        P("role", "tp", "sub"),
    )
    return jax.shard_map(
        per_device, mesh=mesh, in_specs=in_specs, out_specs=P(row, None), check_vma=False
    )
```

```python
import functools
import math

import jax
import jax.numpy as jnp
from jax import lax
from jax.experimental import pallas as pl
from jax.experimental.pallas import tpu as pltpu
from jax.sharding import PartitionSpec as P

D = 3072
HEADS = 24
KV_HEADS = 8
HEAD_DIM = 128
EXPERTS = 4
QBLOCK = 128
LANES = 128
GROUP = HEADS // KV_HEADS
SLOT = 16
PIECES = 2
VMEM_LIMIT = 16 << 20

LOAD_ATTEND = 1
LOAD_STEP = (1, 2)
ORDER = (2, 1, 3)
LOAD_GATE_UP = 2
LOAD_DOWN = 1
WIDTH = 512

VMEM = pl.BlockSpec(memory_space=pltpu.VMEM)
ANY = pl.BlockSpec(memory_space=pltpu.HBM)


def segment(ref, expert, piece):
    depth = ref.shape[1] // PIECES
    return ref.at[expert, pl.ds(piece * depth, depth), :]


def start_loads(places, sources, targets, sems):
    copies = [
        pltpu.make_async_copy(segment(source, *place), target, sems.at[i])
        for i, (place, source, target) in enumerate(zip(places, sources, targets))
    ]
    for copy in copies:
        copy.start()
    return copies


def attend_kernel(*refs, places):
    count = len(places)
    inputs = refs[:13]
    sources = refs[13 : 13 + count]
    x_ref, stream_ref = refs[13 + count : 15 + count]
    scales = refs[15 + count : 18 + count]
    targets = refs[18 + count : 18 + 2 * count]
    scratch = refs[18 + 2 * count :]
    held = scratch[:10]
    q_scr, nk_scr, nv_scr, att_scr, in_sems, load_sems = scratch[10:]
    copies = [
        pltpu.make_async_copy(source, target, in_sems.at[i])
        for i, (source, target) in enumerate(zip(inputs, (*held, *scales)))
    ]
    for copy in copies:
        copy.start()
    loads = start_loads(places, sources, targets, load_sems)
    (
        query_ref,
        new_key_ref,
        new_value_ref,
        lengths_ref,
        cache_key_ref,
        cache_value_ref,
        residual_ref,
        gain_ref,
        ids_ref,
        levels_ref,
    ) = held
    for copy in copies[:4]:
        copy.wait()
    rows, positions, _ = cache_key_ref.shape
    f32 = jnp.float32
    total = KV_HEADS * SLOT
    zeros = jnp.zeros((total, HEAD_DIM), f32)
    q_scr[...] = zeros
    nk_scr[...] = zeros
    nv_scr[...] = zeros
    for j in range(KV_HEADS):
        kv_cols = slice(j * HEAD_DIM, (j + 1) * HEAD_DIM)
        fresh_key = new_key_ref[:, kv_cols].astype(f32)
        fresh_value = new_value_ref[:, kv_cols].astype(f32)
        for g in range(GROUP):
            h = j * GROUP + g
            at = slice(j * SLOT + g * rows, j * SLOT + (g + 1) * rows)
            q_scr[at, :] = query_ref[:, h * HEAD_DIM : (h + 1) * HEAD_DIM].astype(f32)
            nk_scr[at, :] = fresh_key
            nv_scr[at, :] = fresh_value
    queries = q_scr[...]
    factor = 1.0 / math.sqrt(HEAD_DIM)
    fresh_score = jnp.sum(queries * nk_scr[...], axis=1, keepdims=True) * factor
    queries_bf = queries.astype(jnp.bfloat16)
    copies[4].wait()
    keys = cache_key_ref[...].reshape(rows * positions, KV_HEADS * HEAD_DIM)
    scores = jnp.concatenate(
        [
            lax.dot_general(
                queries_bf[j * SLOT : (j + 1) * SLOT],
                keys[:, j * HEAD_DIM : (j + 1) * HEAD_DIM],
                (((1,), (1,)), ((), ())),
                preferred_element_type=f32,
            )
            for j in range(KV_HEADS)
        ],
        axis=0,
    )
    row_of = lax.broadcasted_iota(jnp.int32, (total, positions), 0) % rows
    position = lax.broadcasted_iota(jnp.int32, (total, positions), 1)
    valid = [
        jnp.logical_and(row_of == r, position < lengths_ref[r]) for r in range(rows)
    ]
    pieces = [
        jnp.where(valid[r], scores[:, r * positions : (r + 1) * positions] * factor, -1e30)
        for r in range(rows)
    ]
    peak = functools.reduce(jnp.maximum, pieces)
    peak = jnp.maximum(jnp.max(peak, axis=1, keepdims=True), fresh_score)
    exps = [jnp.where(valid[r], jnp.exp(pieces[r] - peak), 0.0) for r in range(rows)]
    fresh_exp = jnp.exp(fresh_score - peak)
    denominator = jnp.sum(sum(exps[1:], exps[0]), axis=1, keepdims=True) + fresh_exp
    inverse = 1.0 / denominator
    probabilities = jnp.concatenate([(e * inverse).astype(jnp.bfloat16) for e in exps], axis=1)
    fresh_prob = (fresh_exp * inverse).astype(jnp.bfloat16).astype(f32)
    copies[5].wait()
    values = cache_value_ref[...].reshape(rows * positions, KV_HEADS * HEAD_DIM)
    attended = jnp.concatenate(
        [
            jnp.dot(
                probabilities[j * SLOT : (j + 1) * SLOT],
                values[:, j * HEAD_DIM : (j + 1) * HEAD_DIM],
                preferred_element_type=f32,
            )
            for j in range(KV_HEADS)
        ],
        axis=0,
    )
    att_scr[...] = attended + fresh_prob * nv_scr[...]
    for copy in copies[6:10]:
        copy.wait()
    squares = jnp.zeros((rows, HEAD_DIM), f32)
    for j in range(KV_HEADS):
        for g in range(GROUP):
            h = j * GROUP + g
            cols = slice(h * HEAD_DIM, (h + 1) * HEAD_DIM)
            at = slice(j * SLOT + g * rows, j * SLOT + (g + 1) * rows)
            piece = residual_ref[:, cols].astype(f32) + att_scr[at, :]
            stream_ref[:, cols] = piece
            squares = squares + piece * piece
    mean_square = jnp.sum(squares, axis=1, keepdims=True) * (1.0 / D)
    normed = stream_ref[...] * lax.rsqrt(mean_square + 1e-05) * gain_ref[...]
    lane = lax.broadcasted_iota(jnp.int32, (rows, LANES), 1)
    row = lax.broadcasted_iota(jnp.int32, (rows, LANES), 0)
    table = jnp.zeros((rows, LANES), f32)
    for r in range(rows):
        for c in range(2):
            here = jnp.logical_and(row == r, lane == ids_ref[c, r])
            table = jnp.where(here, levels_ref[c, r].astype(f32), table)
    x_ref[...] = jnp.concatenate([normed, table], axis=1).astype(jnp.bfloat16)
    for copy in (*copies[10:], *loads):
        copy.wait()


def spread(scales, columns, dimension):
    blocks = scales.shape[dimension]
    block = lax.broadcasted_iota(jnp.int32, (blocks, columns), 0)
    column = lax.broadcasted_iota(jnp.int32, (blocks, columns), 1)
    pick = (column // QBLOCK == block).astype(jnp.float32)
    return lax.dot_general(
        scales,
        pick,
        (((dimension,), (0,)), ((), ())),
        precision=lax.Precision.HIGHEST,
        preferred_element_type=jnp.float32,
    )


def load_kernel(*refs, places, spreading):
    count = len(places)
    after_ref, scales = refs[0], refs[1 : 1 + 3 * spreading]
    refs = refs[1 + 3 * spreading :]
    sources, refs = refs[:count], refs[count:]
    refs[0][...] = after_ref[...]
    refs = refs[1:]
    rows_refs, refs = refs[: 3 * spreading], refs[3 * spreading :]
    targets, refs = refs[:count], refs[count:]
    load_sems = refs[0]
    loads = start_loads(places, sources, targets, load_sems)
    for i, (source, out_ref) in enumerate(zip(scales, rows_refs)):
        experts, _, columns = out_ref.shape
        for e in range(experts):
            table = source[:, e, :]
            if i == 2:
                out_ref[e] = spread(table, columns, 0)
                continue
            for block in range(columns // QBLOCK):
                at = slice(block * QBLOCK, (block + 1) * QBLOCK)
                wide = (table.shape[0], QBLOCK)
                out_ref[e, :, at] = jnp.broadcast_to(table[:, block : block + 1], wide)
    for load in loads:
        load.wait()


def scaled_product(left, pieces, scales_ref, expert, column, width):
    depth = pieces[0].shape[0] // QBLOCK
    total = None
    for k in range(len(pieces) * depth):
        at = (k % depth) * QBLOCK
        product = jnp.dot(
            left[:, k * QBLOCK : (k + 1) * QBLOCK],
            pieces[k // depth][at : at + QBLOCK, column : column + width],
            preferred_element_type=jnp.float32,
        )
        product = product * scales_ref[expert, k : k + 1, column : column + width]
        total = product if total is None else total + product
    return total


def split_kernel(*refs):
    *pieces, kept_ref, sent_ref = refs
    half = D // 2
    first = lax.axis_index("sub") == 0
    count = pieces[0].shape[0]
    for i, ref in enumerate(pieces):
        at = slice(i * count, (i + 1) * count)
        low, high, table = ref[:, :half], ref[:, half:D], ref[:, D:]
        kept_ref[at, :half] = jnp.where(first, low, high)
        sent_ref[at, :half] = jnp.where(first, high, low)
        kept_ref[at, half:] = table
        sent_ref[at, half:] = table


def chip_rows(kept_ref, other_ref, start, block, columns):
    first = lax.axis_index("sub") == 0
    count = kept_ref.shape[0]
    parts = []
    while block > 0:
        core, row = start // count, start % count
        size = min(block, count - row)
        at = slice(row, row + size)
        pair = kept_ref[at, columns], other_ref[at, columns]
        parts.append(jnp.where(first, pair[core], pair[1 - core]))
        start, block = start + size, block - size
    return parts[0] if len(parts) == 1 else jnp.concatenate(parts, axis=0)


def gate_up_kernel(*refs, expert, places):
    count = len(places)
    kept_ref, other_ref, gate_s_ref, up_s_ref = refs[:4]
    gate, up = refs[4 : 4 + PIECES], [refs[4 + PIECES].at[expert]]
    refs = refs[5 + PIECES :]
    sources, out_ref, targets = refs[:count], refs[count], refs[count + 1 : 2 * count + 1]
    loads = start_loads(places, sources, targets, refs[-1])
    units = gate[0].shape[1]
    depth = gate[0].shape[0] * PIECES
    rows = 2 * kept_ref.shape[0]
    block = min(rows, 64)
    width = min(units, WIDTH)
    for m in range(rows // block):
        at = slice(m * block, (m + 1) * block)
        left = chip_rows(kept_ref, other_ref, m * block, block, slice(0, depth))
        for column in range(0, units, width):
            out_ref[at, column : column + width] = scaled_product(
                left, gate, gate_s_ref, expert, column, width
            ).astype(jnp.bfloat16)
            out_ref[at, units + column : units + column + width] = scaled_product(
                left, up, up_s_ref, expert, column, width
            ).astype(jnp.bfloat16)
    for load in loads:
        load.wait()


def down_kernel(*refs, expert, experts, places):
    count = len(places)
    last = expert == experts - 1
    kept_ref, other_ref, mine, theirs, down_s_ref = refs[:5]
    down, refs = [refs[5].at[expert]], refs[6:]
    before = None
    if expert > 0:
        before, refs = refs[0], refs[1:]
    sources, refs = refs[:count], refs[count:]
    outputs, refs = refs[: 1 + last], refs[1 + last :]
    loads = start_loads(places, sources, refs[:count], refs[count])
    out_ref = refs[count + 1] if last else outputs[0]
    columns = down[0].shape[1]
    units = down[0].shape[0]
    rows, extended = 2 * kept_ref.shape[0], kept_ref.shape[1]
    block = min(rows, 64)
    width = 256
    f32 = jnp.float32
    wanted = lax.axis_index("role") * experts + expert
    for m in range(rows // block):
        at = slice(m * block, (m + 1) * block)
        levels = chip_rows(
            kept_ref, other_ref, m * block, block, slice(extended - LANES, extended)
        ).astype(f32)
        lane = lax.broadcasted_iota(jnp.int32, levels.shape, 1)
        level = jnp.sum(jnp.where(lane == wanted, levels, 0.0), axis=1, keepdims=True)
        share = level / jnp.sum(levels, axis=1, keepdims=True)
        chunks = []
        for u in range(0, units, width):
            gate = mine[at, u : u + width].astype(f32) + theirs[at, u : u + width].astype(f32)
            v = slice(units + u, units + u + width)
            up = mine[at, v].astype(f32) + theirs[at, v].astype(f32)
            silu = gate / (1.0 + jnp.exp(-gate))
            chunks.append((silu * up * share).astype(jnp.bfloat16))
        hidden = jnp.concatenate(chunks, axis=1)
        for column in range(0, columns, width):
            total = scaled_product(hidden, down, down_s_ref, expert, column, width)
            if before is not None:
                total = total + before[at, column : column + width]
            out_ref[at, column : column + width] = total
    if last:
        first = lax.axis_index("sub") == 0
        low, high = out_ref[: rows // 2, :], out_ref[rows // 2 :, :]
        outputs[0][...] = jnp.where(first, low, high).astype(jnp.bfloat16)
        outputs[1][...] = jnp.where(first, high, low).astype(jnp.bfloat16)
    for load in loads:
        load.wait()


def join_kernel(kept_ref, other_ref, *refs):
    half = D // 2
    first = lax.axis_index("sub") == 0
    count = refs[0].shape[0]
    for i, ref in enumerate(refs):
        at = slice(i * count, (i + 1) * count)
        kept, other = kept_ref[at, :], other_ref[at, :]
        ref[:, :half] = jnp.where(first, kept, other)
        ref[:, half:] = jnp.where(first, other, kept)


def finish_kernel(stream_ref, *refs):
    *pieces, out_ref = refs
    total = stream_ref[...]
    for piece in pieces:
        total = total + piece[...].astype(jnp.float32)
    out_ref[...] = total.astype(jnp.bfloat16)


def swap(x, axis, bit):
    if axis is None:
        return lax.ppermute(x, "sub", [(0, 1), (1, 0)])
    count = 2 * lax.axis_size(axis)
    return lax.ppermute(x, (axis, "sub"), [(i, i ^ (2 * bit + 1)) for i in range(count)])


def digits(axis, base):
    size, unit, rounds = lax.axis_size(axis), 1, []
    while unit < size:
        span = min(base, size // unit)
        order = ORDER if span == 4 else (1,)
        rounds.append((axis, tuple(unit * i for i in order)))
        unit *= span
    return rounds


def returned_pieces(pieces, axis, offsets):
    near, *far = pieces
    return [near, *[swap(piece, axis, offset) for piece, offset in zip(far, offsets)]]


def local_call(kernel, outputs, inputs, name):
    return pl.pallas_call(
        kernel,
        out_shape=outputs,
        in_specs=[VMEM] * len(inputs),
        out_specs=jax.tree.map(lambda _: VMEM, outputs),
        compiler_params=pltpu.CompilerParams(vmem_limit_bytes=VMEM_LIMIT),
        name=name,
    )(*inputs)


def add_bf16(pieces):
    total = sum((piece.astype(jnp.float32) for piece in pieces[1:]), pieces[0].astype(jnp.float32))
    return total.astype(jnp.bfloat16)


class Loader:
    def __init__(self, gate, up, down):
        self.experts = gate.shape[0]
        self.arrays = {"gate": gate, "up": up, "down": down}
        self.waiting = [
            (name, e, piece)
            for names in (("gate",),)
            for e in range(self.experts)
            for name in names
            for piece in range(PIECES)
        ]
        self.loaded = {}

    def take(self, count):
        taken, self.waiting = self.waiting[:count], self.waiting[count:]
        return taken

    def missing(self, expert, names):
        return sum(1 for name, e, _ in self.waiting if e == expert and name in names)

    def call(self, kernel, taken, inputs, specs, outputs, scratch, name, cost, **static):
        sources = [self.arrays[segment_name] for segment_name, _, _ in taken]
        shapes = [
            pltpu.VMEM((a.shape[1] // PIECES, a.shape[2]), a.dtype) for a in sources
        ]
        moved = sum(2 * math.prod(shape.shape) for shape in shapes)
        inputs = [
            pltpu.with_memory_space_constraint(x, pltpu.HBM) if spec is ANY else x
            for x, spec in zip(inputs, specs)
        ]
        sources = [pltpu.with_memory_space_constraint(x, pltpu.HBM) for x in sources]
        results = pl.pallas_call(
            functools.partial(kernel, places=tuple((e, p) for _, e, p in taken), **static),
            out_shape=tuple(outputs) + tuple(shapes),
            in_specs=list(specs) + [ANY] * len(taken),
            out_specs=tuple([VMEM] * (len(outputs) + len(taken))),
            scratch_shapes=list(scratch(len(taken))),
            compiler_params=pltpu.CompilerParams(vmem_limit_bytes=VMEM_LIMIT),
            cost_estimate=pl.CostEstimate(
                flops=0, bytes_accessed=cost + moved, transcendentals=0
            ),
            name=name,
        )(*inputs, *sources)
        for at, array in zip(taken, results[len(outputs) :]):
            self.loaded[at] = array
        return results[: len(outputs)]

    def pieces(self, name, expert):
        return [self.loaded[(name, expert, piece)] for piece in range(PIECES)]


def semaphores(count):
    return pltpu.SemaphoreType.DMA((max(count, 1),))


def load_more(loader, taken, after, scales):
    outputs = [jax.ShapeDtypeStruct(after.shape, after.dtype)]
    if scales:
        experts, depth, units = loader.arrays["gate"].shape
        columns = loader.arrays["down"].shape[2]
        outputs += [
            jax.ShapeDtypeStruct((experts, depth // QBLOCK, units), jnp.float32),
            jax.ShapeDtypeStruct((experts, depth // QBLOCK, units), jnp.float32),
            jax.ShapeDtypeStruct((experts, units // QBLOCK, columns), jnp.float32),
        ]
    return loader.call(
        load_kernel,
        taken,
        [after, *scales],
        [VMEM] * (1 + len(scales)),
        outputs,
        lambda count: [semaphores(count)],
        "load",
        1 << 20,
        spreading=1 if scales else 0,
    )


def per_device(
    residual,
    query,
    new_key,
    new_value,
    cache_key,
    cache_value,
    lengths,
    norm_gain,
    expert_ids,
    gate_levels,
    gate_codes,
    gate_scales,
    up_codes,
    up_scales,
    down_codes,
    down_scales,
):
    rows = residual.shape[0]
    half = D // 2
    extended = half + LANES
    experts, _, units = gate_codes.shape
    loader = Loader(gate_codes, up_codes, down_codes)
    inputs = [
        query,
        new_key,
        new_value,
        lengths,
        cache_key,
        cache_value,
        residual,
        norm_gain.reshape(1, D),
        expert_ids.T,
        gate_levels.T,
    ]
    scales = [
        gate_scales.transpose(1, 0, 2),
        up_scales.transpose(1, 0, 2),
        down_scales.transpose(2, 0, 1),
    ]
    stacked = pltpu.VMEM((KV_HEADS * SLOT, HEAD_DIM), jnp.float32)
    held = [
        (pltpu.SMEM if x.dtype == jnp.int32 else pltpu.VMEM)(x.shape, x.dtype) for x in inputs
    ]
    x, stream, *scales = loader.call(
        attend_kernel,
        loader.take(LOAD_ATTEND),
        inputs + scales,
        [ANY] * (len(inputs) + len(scales)),
        [
            jax.ShapeDtypeStruct((rows, D + LANES), jnp.bfloat16),
            jax.ShapeDtypeStruct((rows, D), jnp.float32),
            *[jax.ShapeDtypeStruct(table.shape, table.dtype) for table in scales],
        ],
        lambda count: held + [stacked] * 4 + [semaphores(13), semaphores(count)],
        "attend",
        4 << 20,
    )
    steps = digits("role", 2) + digits("tp", 4)
    spread_scales = None
    near, far = x, []
    for number, (axis, offsets) in enumerate(steps):
        if far:
            near = jnp.concatenate([near, *far], axis=0)
        far = [swap(near, axis, offset) for offset in offsets]
        taken = loader.take(LOAD_STEP[min(number, len(LOAD_STEP) - 1)])
        if spread_scales is None:
            near, *spread_scales = load_more(loader, taken, near, scales)
        elif taken:
            (near,) = load_more(loader, taken, near, [])
    gate_s, up_s, down_s = spread_scales
    count = (1 + len(far)) * near.shape[0]
    piece = jax.ShapeDtypeStruct((count, extended), jnp.bfloat16)
    kept, sent = local_call(split_kernel, (piece, piece), (near, *far), "split")
    other = swap(sent, None, 0)
    parts = []
    before = other
    for e in range(experts):
        missing = loader.missing(e, ("gate",))
        if missing:
            (before,) = load_more(loader, loader.take(missing), before, [])
        (part,) = loader.call(
            gate_up_kernel,
            loader.take(LOAD_GATE_UP),
            [kept, before, gate_s, up_s, *loader.pieces("gate", e), up_codes],
            [VMEM] * (5 + PIECES),
            [jax.ShapeDtypeStruct((2 * count, 2 * units), jnp.bfloat16)],
            lambda loads: [semaphores(loads)],
            "gate_up",
            2 << 20,
            expert=e,
        )
        parts.append((part, swap(part, None, 0)))
        before, _ = lax.optimization_barrier((before, part))
    carried = []
    for e in range(experts):
        last = e == experts - 1
        sums = jax.ShapeDtypeStruct((2 * count, half), jnp.float32)
        returned = jax.ShapeDtypeStruct((count, half), jnp.bfloat16)
        carried = loader.call(
            down_kernel,
            loader.take(LOAD_DOWN),
            [kept, other, *parts[e], down_s, down_codes, *carried],
            [VMEM] * (6 + len(carried)),
            [returned, returned] if last else [sums],
            lambda loads: [semaphores(loads)] + ([pltpu.VMEM(sums.shape, sums.dtype)] if last else []),
            "down",
            4 << 20,
            expert=e,
            experts=experts,
        )
    kept, sent = carried
    axis, offsets = steps[-1]
    parts = 1 + len(offsets)
    piece = jax.ShapeDtypeStruct((count // parts, D), jnp.bfloat16)
    pieces = local_call(join_kernel, (piece,) * parts, (kept, swap(sent, None, 0)), "join")
    for following, _ in zip(reversed(steps[:-1]), steps[1:]):
        carried = add_bf16(returned_pieces(pieces, axis, offsets))
        axis, offsets = following
        pieces = jnp.split(carried, 1 + len(offsets))
    out = jax.ShapeDtypeStruct((rows, D), jnp.bfloat16)
    return local_call(finish_kernel, out, (stream, *returned_pieces(pieces, axis, offsets)), "finish")


def solution(mesh):
    row = ("group", "role", "tp", "sub")
    in_specs = (
        P(row, None),
        P(row, None),
        P(row, None),
        P(row, None),
        P(row, None, None),
        P(row, None, None),
        P(row),
        P(),
        P(row, None),
        P(row, None),
        P("role", "sub", "tp"),
        P("role", "sub", "tp"),
        P("role", "sub", "tp"),
        P("role", "sub", "tp"),
        P("role", "tp", "sub"),
        P("role", "tp", "sub"),
    )
    return jax.shard_map(
        per_device, mesh=mesh, in_specs=in_specs, out_specs=P(row, None), check_vma=False
    )
```

```python
import functools
import math

import jax
import jax.numpy as jnp
from jax import lax
from jax.experimental import pallas as pl
from jax.experimental.pallas import tpu as pltpu
from jax.sharding import PartitionSpec as P

D = 3072
HEADS = 24
KV_HEADS = 8
HEAD_DIM = 128
EXPERTS = 4
QBLOCK = 128
LANES = 128
GROUP = HEADS // KV_HEADS
SLOT = 16
PIECES = 2
VMEM_LIMIT = 16 << 20

LOAD_ATTEND = 0
LOAD_STEP = (1, 3)
ORDER = (2, 1, 3)
RETURN = (3, 2, 1)
LOAD_GATE_UP = 2
LOAD_DOWN = 1
WIDTH = 512

VMEM = pl.BlockSpec(memory_space=pltpu.VMEM)
ANY = pl.BlockSpec(memory_space=pltpu.HBM)


def segment(ref, expert, piece):
    depth = ref.shape[1] // PIECES
    return ref.at[expert, pl.ds(piece * depth, depth), :]


def start_loads(places, sources, targets, sems):
    copies = [
        pltpu.make_async_copy(segment(source, *place), target, sems.at[i])
        for i, (place, source, target) in enumerate(zip(places, sources, targets))
    ]
    for copy in copies:
        copy.start()
    return copies


def attend_kernel(*refs, places):
    count = len(places)
    inputs = refs[:13]
    sources = refs[13 : 13 + count]
    x_ref, stream_ref = refs[13 + count : 15 + count]
    scales = refs[15 + count : 18 + count]
    targets = refs[18 + count : 18 + 2 * count]
    scratch = refs[18 + 2 * count :]
    held = scratch[:10]
    q_scr, nk_scr, nv_scr, att_scr, in_sems, load_sems = scratch[10:]
    copies = [
        pltpu.make_async_copy(source, target, in_sems.at[i])
        for i, (source, target) in enumerate(zip(inputs, (*held, *scales)))
    ]
    for copy in copies:
        copy.start()
    loads = start_loads(places, sources, targets, load_sems)
    (
        query_ref,
        new_key_ref,
        new_value_ref,
        lengths_ref,
        cache_key_ref,
        cache_value_ref,
        residual_ref,
        gain_ref,
        ids_ref,
        levels_ref,
    ) = held
    for copy in copies[:4]:
        copy.wait()
    rows, positions, _ = cache_key_ref.shape
    f32 = jnp.float32
    total = KV_HEADS * SLOT
    zeros = jnp.zeros((total, HEAD_DIM), f32)
    q_scr[...] = zeros
    nk_scr[...] = zeros
    nv_scr[...] = zeros
    for j in range(KV_HEADS):
        kv_cols = slice(j * HEAD_DIM, (j + 1) * HEAD_DIM)
        fresh_key = new_key_ref[:, kv_cols].astype(f32)
        fresh_value = new_value_ref[:, kv_cols].astype(f32)
        for g in range(GROUP):
            h = j * GROUP + g
            at = slice(j * SLOT + g * rows, j * SLOT + (g + 1) * rows)
            q_scr[at, :] = query_ref[:, h * HEAD_DIM : (h + 1) * HEAD_DIM].astype(f32)
            nk_scr[at, :] = fresh_key
            nv_scr[at, :] = fresh_value
    queries = q_scr[...]
    factor = 1.0 / math.sqrt(HEAD_DIM)
    fresh_score = jnp.sum(queries * nk_scr[...], axis=1, keepdims=True) * factor
    queries_bf = queries.astype(jnp.bfloat16)
    copies[4].wait()
    keys = cache_key_ref[...].reshape(rows * positions, KV_HEADS * HEAD_DIM)
    scores = jnp.concatenate(
        [
            lax.dot_general(
                queries_bf[j * SLOT : (j + 1) * SLOT],
                keys[:, j * HEAD_DIM : (j + 1) * HEAD_DIM],
                (((1,), (1,)), ((), ())),
                preferred_element_type=f32,
            )
            for j in range(KV_HEADS)
        ],
        axis=0,
    )
    row_of = lax.broadcasted_iota(jnp.int32, (total, positions), 0) % rows
    position = lax.broadcasted_iota(jnp.int32, (total, positions), 1)
    valid = [
        jnp.logical_and(row_of == r, position < lengths_ref[r]) for r in range(rows)
    ]
    pieces = [
        jnp.where(valid[r], scores[:, r * positions : (r + 1) * positions] * factor, -1e30)
        for r in range(rows)
    ]
    peak = functools.reduce(jnp.maximum, pieces)
    peak = jnp.maximum(jnp.max(peak, axis=1, keepdims=True), fresh_score)
    exps = [jnp.where(valid[r], jnp.exp(pieces[r] - peak), 0.0) for r in range(rows)]
    fresh_exp = jnp.exp(fresh_score - peak)
    denominator = jnp.sum(sum(exps[1:], exps[0]), axis=1, keepdims=True) + fresh_exp
    inverse = 1.0 / denominator
    probabilities = jnp.concatenate([(e * inverse).astype(jnp.bfloat16) for e in exps], axis=1)
    fresh_prob = (fresh_exp * inverse).astype(jnp.bfloat16).astype(f32)
    copies[5].wait()
    values = cache_value_ref[...].reshape(rows * positions, KV_HEADS * HEAD_DIM)
    attended = jnp.concatenate(
        [
            jnp.dot(
                probabilities[j * SLOT : (j + 1) * SLOT],
                values[:, j * HEAD_DIM : (j + 1) * HEAD_DIM],
                preferred_element_type=f32,
            )
            for j in range(KV_HEADS)
        ],
        axis=0,
    )
    att_scr[...] = attended + fresh_prob * nv_scr[...]
    for copy in copies[6:10]:
        copy.wait()
    squares = jnp.zeros((rows, HEAD_DIM), f32)
    for j in range(KV_HEADS):
        for g in range(GROUP):
            h = j * GROUP + g
            cols = slice(h * HEAD_DIM, (h + 1) * HEAD_DIM)
            at = slice(j * SLOT + g * rows, j * SLOT + (g + 1) * rows)
            piece = residual_ref[:, cols].astype(f32) + att_scr[at, :]
            stream_ref[:, cols] = piece
            squares = squares + piece * piece
    mean_square = jnp.sum(squares, axis=1, keepdims=True) * (1.0 / D)
    normed = stream_ref[...] * lax.rsqrt(mean_square + 1e-05) * gain_ref[...]
    lane = lax.broadcasted_iota(jnp.int32, (rows, LANES), 1)
    row = lax.broadcasted_iota(jnp.int32, (rows, LANES), 0)
    table = jnp.zeros((rows, LANES), f32)
    for r in range(rows):
        for c in range(2):
            here = jnp.logical_and(row == r, lane == ids_ref[c, r])
            table = jnp.where(here, levels_ref[c, r].astype(f32), table)
    x_ref[...] = jnp.concatenate([normed, table], axis=1).astype(jnp.bfloat16)
    for copy in (*copies[10:], *loads):
        copy.wait()


def spread(scales, columns, dimension):
    blocks = scales.shape[dimension]
    block = lax.broadcasted_iota(jnp.int32, (blocks, columns), 0)
    column = lax.broadcasted_iota(jnp.int32, (blocks, columns), 1)
    pick = (column // QBLOCK == block).astype(jnp.float32)
    return lax.dot_general(
        scales,
        pick,
        (((dimension,), (0,)), ((), ())),
        precision=lax.Precision.HIGHEST,
        preferred_element_type=jnp.float32,
    )


def load_kernel(*refs, places, spreading):
    count = len(places)
    after_ref, scales = refs[0], refs[1 : 1 + 3 * spreading]
    refs = refs[1 + 3 * spreading :]
    sources, refs = refs[:count], refs[count:]
    refs[0][...] = after_ref[...]
    refs = refs[1:]
    rows_refs, refs = refs[: 3 * spreading], refs[3 * spreading :]
    targets, refs = refs[:count], refs[count:]
    load_sems = refs[0]
    loads = start_loads(places, sources, targets, load_sems)
    for i, (source, out_ref) in enumerate(zip(scales, rows_refs)):
        experts, _, columns = out_ref.shape
        for e in range(experts):
            table = source[:, e, :]
            if i == 2:
                out_ref[e] = spread(table, columns, 0)
                continue
            for block in range(columns // QBLOCK):
                at = slice(block * QBLOCK, (block + 1) * QBLOCK)
                wide = (table.shape[0], QBLOCK)
                out_ref[e, :, at] = jnp.broadcast_to(table[:, block : block + 1], wide)
    for load in loads:
        load.wait()


def scaled_product(left, pieces, scales_ref, expert, column, width):
    depth = pieces[0].shape[0] // QBLOCK
    total = None
    for k in range(len(pieces) * depth):
        at = (k % depth) * QBLOCK
        product = jnp.dot(
            left[:, k * QBLOCK : (k + 1) * QBLOCK],
            pieces[k // depth][at : at + QBLOCK, column : column + width],
            preferred_element_type=jnp.float32,
        )
        product = product * scales_ref[expert, k : k + 1, column : column + width]
        total = product if total is None else total + product
    return total


def split_kernel(*refs):
    *pieces, kept_ref, sent_ref = refs
    half = D // 2
    first = lax.axis_index("sub") == 0
    count = pieces[0].shape[0]
    for i, ref in enumerate(pieces):
        at = slice(i * count, (i + 1) * count)
        low, high, table = ref[:, :half], ref[:, half:D], ref[:, D:]
        kept_ref[at, :half] = jnp.where(first, low, high)
        sent_ref[at, :half] = jnp.where(first, high, low)
        kept_ref[at, half:] = table
        sent_ref[at, half:] = table


def chip_rows(kept_ref, other_ref, start, block, columns):
    first = lax.axis_index("sub") == 0
    count = kept_ref.shape[0]
    parts = []
    while block > 0:
        core, row = start // count, start % count
        size = min(block, count - row)
        at = slice(row, row + size)
        pair = kept_ref[at, columns], other_ref[at, columns]
        parts.append(jnp.where(first, pair[core], pair[1 - core]))
        start, block = start + size, block - size
    return parts[0] if len(parts) == 1 else jnp.concatenate(parts, axis=0)


def gate_up_kernel(*refs, expert, places):
    count = len(places)
    kept_ref, other_ref, gate_s_ref, up_s_ref = refs[:4]
    gate, up = refs[4 : 4 + PIECES], [refs[4 + PIECES].at[expert]]
    refs = refs[5 + PIECES :]
    sources, out_ref, targets = refs[:count], refs[count], refs[count + 1 : 2 * count + 1]
    loads = start_loads(places, sources, targets, refs[-1])
    units = gate[0].shape[1]
    depth = gate[0].shape[0] * PIECES
    rows = 2 * kept_ref.shape[0]
    block = min(rows, 64)
    width = min(units, WIDTH)
    for m in range(rows // block):
        at = slice(m * block, (m + 1) * block)
        left = chip_rows(kept_ref, other_ref, m * block, block, slice(0, depth))
        for column in range(0, units, width):
            out_ref[at, column : column + width] = scaled_product(
                left, gate, gate_s_ref, expert, column, width
            ).astype(jnp.bfloat16)
            out_ref[at, units + column : units + column + width] = scaled_product(
                left, up, up_s_ref, expert, column, width
            ).astype(jnp.bfloat16)
    for load in loads:
        load.wait()


def down_kernel(*refs, expert, experts, places):
    count = len(places)
    last = expert == experts - 1
    kept_ref, other_ref, mine, theirs, down_s_ref = refs[:5]
    down, refs = [refs[5].at[expert]], refs[6:]
    before = None
    if expert > 0:
        before, refs = refs[0], refs[1:]
    sources, refs = refs[:count], refs[count:]
    outputs, refs = refs[: 1 + last], refs[1 + last :]
    loads = start_loads(places, sources, refs[:count], refs[count])
    out_ref = refs[count + 1] if last else outputs[0]
    columns = down[0].shape[1]
    units = down[0].shape[0]
    rows, extended = 2 * kept_ref.shape[0], kept_ref.shape[1]
    block = min(rows, 64)
    width = 256
    f32 = jnp.float32
    wanted = lax.axis_index("role") * experts + expert
    for m in range(rows // block):
        at = slice(m * block, (m + 1) * block)
        levels = chip_rows(
            kept_ref, other_ref, m * block, block, slice(extended - LANES, extended)
        ).astype(f32)
        lane = lax.broadcasted_iota(jnp.int32, levels.shape, 1)
        level = jnp.sum(jnp.where(lane == wanted, levels, 0.0), axis=1, keepdims=True)
        share = level / jnp.sum(levels, axis=1, keepdims=True)
        chunks = []
        for u in range(0, units, width):
            gate = mine[at, u : u + width].astype(f32) + theirs[at, u : u + width].astype(f32)
            v = slice(units + u, units + u + width)
            up = mine[at, v].astype(f32) + theirs[at, v].astype(f32)
            silu = gate / (1.0 + jnp.exp(-gate))
            chunks.append((silu * up * share).astype(jnp.bfloat16))
        hidden = jnp.concatenate(chunks, axis=1)
        for column in range(0, columns, width):
            total = scaled_product(hidden, down, down_s_ref, expert, column, width)
            if before is not None:
                total = total + before[at, column : column + width]
            out_ref[at, column : column + width] = total
    if last:
        first = lax.axis_index("sub") == 0
        low, high = out_ref[: rows // 2, :], out_ref[rows // 2 :, :]
        outputs[0][...] = jnp.where(first, low, high).astype(jnp.bfloat16)
        outputs[1][...] = jnp.where(first, high, low).astype(jnp.bfloat16)
    for load in loads:
        load.wait()


def join_kernel(kept_ref, other_ref, *refs, blocks):
    half = D // 2
    first = lax.axis_index("sub") == 0
    count = refs[0].shape[0]
    for block, ref in zip(blocks, refs):
        at = slice(block * count, (block + 1) * count)
        kept, other = kept_ref[at, :], other_ref[at, :]
        ref[:, :half] = jnp.where(first, kept, other)
        ref[:, half:] = jnp.where(first, other, kept)


def finish_kernel(stream_ref, *refs):
    *pieces, out_ref = refs
    total = stream_ref[...]
    for piece in pieces:
        total = total + piece[...].astype(jnp.float32)
    out_ref[...] = total.astype(jnp.bfloat16)


def swap(x, axis, bit):
    if axis is None:
        return lax.ppermute(x, "sub", [(0, 1), (1, 0)])
    count = 2 * lax.axis_size(axis)
    return lax.ppermute(x, (axis, "sub"), [(i, i ^ (2 * bit + 1)) for i in range(count)])


def digits(axis, base):
    size, unit, rounds = lax.axis_size(axis), 1, []
    while unit < size:
        span = min(base, size // unit)
        order = ORDER if span == 4 else (1,)
        rounds.append((axis, tuple(unit * i for i in order)))
        unit *= span
    return rounds


def returned_pieces(pieces, axis, offsets):
    near, *far = pieces
    return [near, *[swap(piece, axis, offset) for piece, offset in zip(far, offsets)]]


def local_call(kernel, outputs, inputs, name):
    return pl.pallas_call(
        kernel,
        out_shape=outputs,
        in_specs=[VMEM] * len(inputs),
        out_specs=jax.tree.map(lambda _: VMEM, outputs),
        compiler_params=pltpu.CompilerParams(vmem_limit_bytes=VMEM_LIMIT),
        name=name,
    )(*inputs)


def add_bf16(pieces):
    total = sum((piece.astype(jnp.float32) for piece in pieces[1:]), pieces[0].astype(jnp.float32))
    return total.astype(jnp.bfloat16)


class Loader:
    def __init__(self, gate, up, down):
        self.experts = gate.shape[0]
        self.arrays = {"gate": gate, "up": up, "down": down}
        self.waiting = [
            (name, e, piece)
            for names in (("gate",),)
            for e in range(self.experts)
            for name in names
            for piece in range(PIECES)
        ]
        self.loaded = {}

    def take(self, count):
        taken, self.waiting = self.waiting[:count], self.waiting[count:]
        return taken

    def missing(self, expert, names):
        return sum(1 for name, e, _ in self.waiting if e == expert and name in names)

    def call(self, kernel, taken, inputs, specs, outputs, scratch, name, cost, **static):
        sources = [self.arrays[segment_name] for segment_name, _, _ in taken]
        shapes = [
            pltpu.VMEM((a.shape[1] // PIECES, a.shape[2]), a.dtype) for a in sources
        ]
        moved = sum(2 * math.prod(shape.shape) for shape in shapes)
        inputs = [
            pltpu.with_memory_space_constraint(x, pltpu.HBM) if spec is ANY else x
            for x, spec in zip(inputs, specs)
        ]
        sources = [pltpu.with_memory_space_constraint(x, pltpu.HBM) for x in sources]
        results = pl.pallas_call(
            functools.partial(kernel, places=tuple((e, p) for _, e, p in taken), **static),
            out_shape=tuple(outputs) + tuple(shapes),
            in_specs=list(specs) + [ANY] * len(taken),
            out_specs=tuple([VMEM] * (len(outputs) + len(taken))),
            scratch_shapes=list(scratch(len(taken))),
            compiler_params=pltpu.CompilerParams(vmem_limit_bytes=VMEM_LIMIT),
            cost_estimate=pl.CostEstimate(
                flops=0, bytes_accessed=cost + moved, transcendentals=0
            ),
            name=name,
        )(*inputs, *sources)
        for at, array in zip(taken, results[len(outputs) :]):
            self.loaded[at] = array
        return results[: len(outputs)]

    def pieces(self, name, expert):
        return [self.loaded[(name, expert, piece)] for piece in range(PIECES)]


def semaphores(count):
    return pltpu.SemaphoreType.DMA((max(count, 1),))


def load_more(loader, taken, after, scales):
    outputs = [jax.ShapeDtypeStruct(after.shape, after.dtype)]
    if scales:
        experts, depth, units = loader.arrays["gate"].shape
        columns = loader.arrays["down"].shape[2]
        outputs += [
            jax.ShapeDtypeStruct((experts, depth // QBLOCK, units), jnp.float32),
            jax.ShapeDtypeStruct((experts, depth // QBLOCK, units), jnp.float32),
            jax.ShapeDtypeStruct((experts, units // QBLOCK, columns), jnp.float32),
        ]
    return loader.call(
        load_kernel,
        taken,
        [after, *scales],
        [VMEM] * (1 + len(scales)),
        outputs,
        lambda count: [semaphores(count)],
        "load",
        1 << 20,
        spreading=1 if scales else 0,
    )


def per_device(
    residual,
    query,
    new_key,
    new_value,
    cache_key,
    cache_value,
    lengths,
    norm_gain,
    expert_ids,
    gate_levels,
    gate_codes,
    gate_scales,
    up_codes,
    up_scales,
    down_codes,
    down_scales,
):
    rows = residual.shape[0]
    half = D // 2
    extended = half + LANES
    experts, _, units = gate_codes.shape
    loader = Loader(gate_codes, up_codes, down_codes)
    inputs = [
        query,
        new_key,
        new_value,
        lengths,
        cache_key,
        cache_value,
        residual,
        norm_gain.reshape(1, D),
        expert_ids.T,
        gate_levels.T,
    ]
    scales = [
        gate_scales.transpose(1, 0, 2),
        up_scales.transpose(1, 0, 2),
        down_scales.transpose(2, 0, 1),
    ]
    stacked = pltpu.VMEM((KV_HEADS * SLOT, HEAD_DIM), jnp.float32)
    held = [
        (pltpu.SMEM if x.dtype == jnp.int32 else pltpu.VMEM)(x.shape, x.dtype) for x in inputs
    ]
    x, stream, *scales = loader.call(
        attend_kernel,
        loader.take(LOAD_ATTEND),
        inputs + scales,
        [ANY] * (len(inputs) + len(scales)),
        [
            jax.ShapeDtypeStruct((rows, D + LANES), jnp.bfloat16),
            jax.ShapeDtypeStruct((rows, D), jnp.float32),
            *[jax.ShapeDtypeStruct(table.shape, table.dtype) for table in scales],
        ],
        lambda count: held + [stacked] * 4 + [semaphores(13), semaphores(count)],
        "attend",
        4 << 20,
    )
    steps = digits("role", 2) + digits("tp", 4)
    spread_scales = None
    near, far = x, []
    for number, (axis, offsets) in enumerate(steps):
        if far:
            near = jnp.concatenate([near, *far], axis=0)
        far = [swap(near, axis, offset) for offset in offsets]
        taken = loader.take(LOAD_STEP[min(number, len(LOAD_STEP) - 1)])
        if spread_scales is None:
            near, *spread_scales = load_more(loader, taken, near, scales)
        elif taken:
            (near,) = load_more(loader, taken, near, [])
    gate_s, up_s, down_s = spread_scales
    count = (1 + len(far)) * near.shape[0]
    piece = jax.ShapeDtypeStruct((count, extended), jnp.bfloat16)
    kept, sent = local_call(split_kernel, (piece, piece), (near, *far), "split")
    other = swap(sent, None, 0)
    parts = []
    before = other
    for e in range(experts):
        missing = loader.missing(e, ("gate",))
        if missing:
            (before,) = load_more(loader, loader.take(missing), before, [])
        (part,) = loader.call(
            gate_up_kernel,
            loader.take(LOAD_GATE_UP),
            [kept, before, gate_s, up_s, *loader.pieces("gate", e), up_codes],
            [VMEM] * (5 + PIECES),
            [jax.ShapeDtypeStruct((2 * count, 2 * units), jnp.bfloat16)],
            lambda loads: [semaphores(loads)],
            "gate_up",
            2 << 20,
            expert=e,
        )
        parts.append((part, swap(part, None, 0)))
        before, _ = lax.optimization_barrier((before, part))
    carried = []
    for e in range(experts):
        last = e == experts - 1
        sums = jax.ShapeDtypeStruct((2 * count, half), jnp.float32)
        returned = jax.ShapeDtypeStruct((count, half), jnp.bfloat16)
        carried = loader.call(
            down_kernel,
            loader.take(LOAD_DOWN),
            [kept, other, *parts[e], down_s, down_codes, *carried],
            [VMEM] * (6 + len(carried)),
            [returned, returned] if last else [sums],
            lambda loads: [semaphores(loads)] + ([pltpu.VMEM(sums.shape, sums.dtype)] if last else []),
            "down",
            4 << 20,
            expert=e,
            experts=experts,
        )
    kept, sent = carried
    axis, offsets = steps[-1]
    parts = 1 + len(offsets)
    piece = jax.ShapeDtypeStruct((count // parts, D), jnp.bfloat16)
    blocks = [0, *RETURN] if parts == 4 else list(range(parts))
    offsets = tuple(offsets[block - 1] for block in blocks[1:])
    joined = functools.partial(join_kernel, blocks=tuple(blocks))
    pieces = local_call(joined, (piece,) * parts, (kept, swap(sent, None, 0)), "join")
    for following, _ in zip(reversed(steps[:-1]), steps[1:]):
        carried = add_bf16(returned_pieces(pieces, axis, offsets))
        axis, offsets = following
        pieces = jnp.split(carried, 1 + len(offsets))
    out = jax.ShapeDtypeStruct((rows, D), jnp.bfloat16)
    return local_call(finish_kernel, out, (stream, *returned_pieces(pieces, axis, offsets)), "finish")


def solution(mesh):
    row = ("group", "role", "tp", "sub")
    in_specs = (
        P(row, None),
        P(row, None),
        P(row, None),
        P(row, None),
        P(row, None, None),
        P(row, None, None),
        P(row),
        P(),
        P(row, None),
        P(row, None),
        P("role", "sub", "tp"),
        P("role", "sub", "tp"),
        P("role", "sub", "tp"),
        P("role", "sub", "tp"),
        P("role", "tp", "sub"),
        P("role", "tp", "sub"),
    )
    return jax.shard_map(
        per_device, mesh=mesh, in_specs=in_specs, out_specs=P(row, None), check_vma=False
    )
```

```python
import functools
import math

import jax
import jax.numpy as jnp
from jax import lax
from jax.experimental import pallas as pl
from jax.experimental.pallas import tpu as pltpu
from jax.sharding import PartitionSpec as P

D = 3072
HEADS = 24
KV_HEADS = 8
HEAD_DIM = 128
EXPERTS = 4
QBLOCK = 128
LANES = 128
GROUP = HEADS // KV_HEADS
SLOT = 16
PIECES = 2
VMEM_LIMIT = 16 << 20

LOAD_ATTEND = 0
LOAD_STEP = (2, 2)
ORDER = ((1, 0), (0, 1), (1, 1))
RETURN = (3, 1, 2)
LOAD_GATE_UP = 2
LOAD_DOWN = 1
WIDTH = 512

VMEM = pl.BlockSpec(memory_space=pltpu.VMEM)
ANY = pl.BlockSpec(memory_space=pltpu.HBM)


def segment(ref, expert, piece):
    depth = ref.shape[1] // PIECES
    return ref.at[expert, pl.ds(piece * depth, depth), :]


def start_loads(places, sources, targets, sems):
    copies = [
        pltpu.make_async_copy(segment(source, *place), target, sems.at[i])
        for i, (place, source, target) in enumerate(zip(places, sources, targets))
    ]
    for copy in copies:
        copy.start()
    return copies


def attend_kernel(*refs, places):
    count = len(places)
    inputs = refs[:13]
    sources = refs[13 : 13 + count]
    x_ref, stream_ref = refs[13 + count : 15 + count]
    scales = refs[15 + count : 18 + count]
    targets = refs[18 + count : 18 + 2 * count]
    scratch = refs[18 + 2 * count :]
    held = scratch[:10]
    q_scr, nk_scr, nv_scr, att_scr, in_sems, load_sems = scratch[10:]
    copies = [
        pltpu.make_async_copy(source, target, in_sems.at[i])
        for i, (source, target) in enumerate(zip(inputs, (*held, *scales)))
    ]
    for copy in copies:
        copy.start()
    loads = start_loads(places, sources, targets, load_sems)
    (
        query_ref,
        new_key_ref,
        new_value_ref,
        lengths_ref,
        cache_key_ref,
        cache_value_ref,
        residual_ref,
        gain_ref,
        ids_ref,
        levels_ref,
    ) = held
    for copy in copies[:4]:
        copy.wait()
    rows, positions, _ = cache_key_ref.shape
    f32 = jnp.float32
    total = KV_HEADS * SLOT
    zeros = jnp.zeros((total, HEAD_DIM), f32)
    q_scr[...] = zeros
    nk_scr[...] = zeros
    nv_scr[...] = zeros
    for j in range(KV_HEADS):
        kv_cols = slice(j * HEAD_DIM, (j + 1) * HEAD_DIM)
        fresh_key = new_key_ref[:, kv_cols].astype(f32)
        fresh_value = new_value_ref[:, kv_cols].astype(f32)
        for g in range(GROUP):
            h = j * GROUP + g
            at = slice(j * SLOT + g * rows, j * SLOT + (g + 1) * rows)
            q_scr[at, :] = query_ref[:, h * HEAD_DIM : (h + 1) * HEAD_DIM].astype(f32)
            nk_scr[at, :] = fresh_key
            nv_scr[at, :] = fresh_value
    queries = q_scr[...]
    factor = 1.0 / math.sqrt(HEAD_DIM)
    fresh_score = jnp.sum(queries * nk_scr[...], axis=1, keepdims=True) * factor
    queries_bf = queries.astype(jnp.bfloat16)
    copies[4].wait()
    keys = cache_key_ref[...].reshape(rows * positions, KV_HEADS * HEAD_DIM)
    scores = jnp.concatenate(
        [
            lax.dot_general(
                queries_bf[j * SLOT : (j + 1) * SLOT],
                keys[:, j * HEAD_DIM : (j + 1) * HEAD_DIM],
                (((1,), (1,)), ((), ())),
                preferred_element_type=f32,
            )
            for j in range(KV_HEADS)
        ],
        axis=0,
    )
    row_of = lax.broadcasted_iota(jnp.int32, (total, positions), 0) % rows
    position = lax.broadcasted_iota(jnp.int32, (total, positions), 1)
    valid = [
        jnp.logical_and(row_of == r, position < lengths_ref[r]) for r in range(rows)
    ]
    pieces = [
        jnp.where(valid[r], scores[:, r * positions : (r + 1) * positions] * factor, -1e30)
        for r in range(rows)
    ]
    peak = functools.reduce(jnp.maximum, pieces)
    peak = jnp.maximum(jnp.max(peak, axis=1, keepdims=True), fresh_score)
    exps = [jnp.where(valid[r], jnp.exp(pieces[r] - peak), 0.0) for r in range(rows)]
    fresh_exp = jnp.exp(fresh_score - peak)
    denominator = jnp.sum(sum(exps[1:], exps[0]), axis=1, keepdims=True) + fresh_exp
    inverse = 1.0 / denominator
    probabilities = jnp.concatenate([(e * inverse).astype(jnp.bfloat16) for e in exps], axis=1)
    fresh_prob = (fresh_exp * inverse).astype(jnp.bfloat16).astype(f32)
    copies[5].wait()
    values = cache_value_ref[...].reshape(rows * positions, KV_HEADS * HEAD_DIM)
    attended = jnp.concatenate(
        [
            jnp.dot(
                probabilities[j * SLOT : (j + 1) * SLOT],
                values[:, j * HEAD_DIM : (j + 1) * HEAD_DIM],
                preferred_element_type=f32,
            )
            for j in range(KV_HEADS)
        ],
        axis=0,
    )
    att_scr[...] = attended + fresh_prob * nv_scr[...]
    for copy in copies[6:10]:
        copy.wait()
    squares = jnp.zeros((rows, HEAD_DIM), f32)
    for j in range(KV_HEADS):
        for g in range(GROUP):
            h = j * GROUP + g
            cols = slice(h * HEAD_DIM, (h + 1) * HEAD_DIM)
            at = slice(j * SLOT + g * rows, j * SLOT + (g + 1) * rows)
            piece = residual_ref[:, cols].astype(f32) + att_scr[at, :]
            stream_ref[:, cols] = piece
            squares = squares + piece * piece
    mean_square = jnp.sum(squares, axis=1, keepdims=True) * (1.0 / D)
    normed = stream_ref[...] * lax.rsqrt(mean_square + 1e-05) * gain_ref[...]
    lane = lax.broadcasted_iota(jnp.int32, (rows, LANES), 1)
    row = lax.broadcasted_iota(jnp.int32, (rows, LANES), 0)
    table = jnp.zeros((rows, LANES), f32)
    for r in range(rows):
        for c in range(2):
            here = jnp.logical_and(row == r, lane == ids_ref[c, r])
            table = jnp.where(here, levels_ref[c, r].astype(f32), table)
    x_ref[...] = jnp.concatenate([normed, table], axis=1).astype(jnp.bfloat16)
    for copy in (*copies[10:], *loads):
        copy.wait()


def spread(scales, columns, dimension):
    blocks = scales.shape[dimension]
    block = lax.broadcasted_iota(jnp.int32, (blocks, columns), 0)
    column = lax.broadcasted_iota(jnp.int32, (blocks, columns), 1)
    pick = (column // QBLOCK == block).astype(jnp.float32)
    return lax.dot_general(
        scales,
        pick,
        (((dimension,), (0,)), ((), ())),
        precision=lax.Precision.HIGHEST,
        preferred_element_type=jnp.float32,
    )


def load_kernel(*refs, places, spreading):
    count = len(places)
    after_ref, scales = refs[0], refs[1 : 1 + 3 * spreading]
    refs = refs[1 + 3 * spreading :]
    sources, refs = refs[:count], refs[count:]
    refs[0][...] = after_ref[...]
    refs = refs[1:]
    rows_refs, refs = refs[: 3 * spreading], refs[3 * spreading :]
    targets, refs = refs[:count], refs[count:]
    load_sems = refs[0]
    loads = start_loads(places, sources, targets, load_sems)
    for i, (source, out_ref) in enumerate(zip(scales, rows_refs)):
        experts, _, columns = out_ref.shape
        for e in range(experts):
            table = source[:, e, :]
            if i == 2:
                out_ref[e] = spread(table, columns, 0)
                continue
            for block in range(columns // QBLOCK):
                at = slice(block * QBLOCK, (block + 1) * QBLOCK)
                wide = (table.shape[0], QBLOCK)
                out_ref[e, :, at] = jnp.broadcast_to(table[:, block : block + 1], wide)
    for load in loads:
        load.wait()


def scaled_product(left, pieces, scales_ref, expert, column, width):
    depth = pieces[0].shape[0] // QBLOCK
    total = None
    for k in range(len(pieces) * depth):
        at = (k % depth) * QBLOCK
        product = jnp.dot(
            left[:, k * QBLOCK : (k + 1) * QBLOCK],
            pieces[k // depth][at : at + QBLOCK, column : column + width],
            preferred_element_type=jnp.float32,
        )
        product = product * scales_ref[expert, k : k + 1, column : column + width]
        total = product if total is None else total + product
    return total


def split_kernel(*refs):
    *pieces, kept_ref, sent_ref = refs
    half = D // 2
    first = lax.axis_index("sub") == 0
    count = pieces[0].shape[0]
    for i, ref in enumerate(pieces):
        at = slice(i * count, (i + 1) * count)
        low, high, table = ref[:, :half], ref[:, half:D], ref[:, D:]
        kept_ref[at, :half] = jnp.where(first, low, high)
        sent_ref[at, :half] = jnp.where(first, high, low)
        kept_ref[at, half:] = table
        sent_ref[at, half:] = table


def chip_rows(kept_ref, other_ref, start, block, columns):
    first = lax.axis_index("sub") == 0
    count = kept_ref.shape[0]
    parts = []
    while block > 0:
        core, row = start // count, start % count
        size = min(block, count - row)
        at = slice(row, row + size)
        pair = kept_ref[at, columns], other_ref[at, columns]
        parts.append(jnp.where(first, pair[core], pair[1 - core]))
        start, block = start + size, block - size
    return parts[0] if len(parts) == 1 else jnp.concatenate(parts, axis=0)


def gate_up_kernel(*refs, expert, places):
    count = len(places)
    kept_ref, other_ref, gate_s_ref, up_s_ref = refs[:4]
    gate, up = refs[4 : 4 + PIECES], [refs[4 + PIECES].at[expert]]
    refs = refs[5 + PIECES :]
    sources, out_ref, targets = refs[:count], refs[count], refs[count + 1 : 2 * count + 1]
    loads = start_loads(places, sources, targets, refs[-1])
    units = gate[0].shape[1]
    depth = gate[0].shape[0] * PIECES
    rows = 2 * kept_ref.shape[0]
    block = min(rows, 64)
    width = min(units, WIDTH)
    for m in range(rows // block):
        at = slice(m * block, (m + 1) * block)
        left = chip_rows(kept_ref, other_ref, m * block, block, slice(0, depth))
        for column in range(0, units, width):
            out_ref[at, column : column + width] = scaled_product(
                left, gate, gate_s_ref, expert, column, width
            ).astype(jnp.bfloat16)
            out_ref[at, units + column : units + column + width] = scaled_product(
                left, up, up_s_ref, expert, column, width
            ).astype(jnp.bfloat16)
    for load in loads:
        load.wait()


def down_kernel(*refs, expert, experts, places):
    count = len(places)
    last = expert == experts - 1
    kept_ref, other_ref, mine, theirs, down_s_ref = refs[:5]
    down, refs = [refs[5].at[expert]], refs[6:]
    before = None
    if expert > 0:
        before, refs = refs[0], refs[1:]
    sources, refs = refs[:count], refs[count:]
    outputs, refs = refs[: 1 + last], refs[1 + last :]
    loads = start_loads(places, sources, refs[:count], refs[count])
    out_ref = refs[count + 1] if last else outputs[0]
    columns = down[0].shape[1]
    units = down[0].shape[0]
    rows, extended = 2 * kept_ref.shape[0], kept_ref.shape[1]
    block = min(rows, 64)
    width = 256
    f32 = jnp.float32
    wanted = lax.axis_index("role") * experts + expert
    for m in range(rows // block):
        at = slice(m * block, (m + 1) * block)
        levels = chip_rows(
            kept_ref, other_ref, m * block, block, slice(extended - LANES, extended)
        ).astype(f32)
        lane = lax.broadcasted_iota(jnp.int32, levels.shape, 1)
        level = jnp.sum(jnp.where(lane == wanted, levels, 0.0), axis=1, keepdims=True)
        share = level / jnp.sum(levels, axis=1, keepdims=True)
        chunks = []
        for u in range(0, units, width):
            gate = mine[at, u : u + width].astype(f32) + theirs[at, u : u + width].astype(f32)
            v = slice(units + u, units + u + width)
            up = mine[at, v].astype(f32) + theirs[at, v].astype(f32)
            silu = gate / (1.0 + jnp.exp(-gate))
            chunks.append((silu * up * share).astype(jnp.bfloat16))
        hidden = jnp.concatenate(chunks, axis=1)
        for column in range(0, columns, width):
            total = scaled_product(hidden, down, down_s_ref, expert, column, width)
            if before is not None:
                total = total + before[at, column : column + width]
            out_ref[at, column : column + width] = total
    if last:
        first = lax.axis_index("sub") == 0
        low, high = out_ref[: rows // 2, :], out_ref[rows // 2 :, :]
        outputs[0][...] = jnp.where(first, low, high).astype(jnp.bfloat16)
        outputs[1][...] = jnp.where(first, high, low).astype(jnp.bfloat16)
    for load in loads:
        load.wait()


def join_kernel(kept_ref, other_ref, *refs, blocks):
    half = D // 2
    first = lax.axis_index("sub") == 0
    count = refs[0].shape[0]
    for block, ref in zip(blocks, refs):
        at = slice(block * count, (block + 1) * count)
        kept, other = kept_ref[at, :], other_ref[at, :]
        ref[:, :half] = jnp.where(first, kept, other)
        ref[:, half:] = jnp.where(first, other, kept)


def finish_kernel(stream_ref, *refs):
    *pieces, out_ref = refs
    total = stream_ref[...]
    for piece in pieces:
        total = total + piece[...].astype(jnp.float32)
    out_ref[...] = total.astype(jnp.bfloat16)


def swap(x, offset):
    if offset is None:
        return lax.ppermute(x, "sub", [(0, 1), (1, 0)])
    roles, columns = lax.axis_size("role"), lax.axis_size("tp")
    flip = 2 * (offset[0] * columns + offset[1]) + 1
    pairs = [(i, i ^ flip) for i in range(2 * roles * columns)]
    return lax.ppermute(x, ("role", "tp", "sub"), pairs)


def rounds():
    roles, columns = lax.axis_size("role"), lax.axis_size("tp")
    bits = [1 << b for b in reversed(range(1, max(roles, columns).bit_length()))]
    steps = [((0, bit),) for bit in bits if bit < columns]
    steps += [((bit, 0),) for bit in bits if bit < roles]
    lowest = [pair for pair in ORDER if pair[0] < roles and pair[1] < columns]
    return steps + [tuple(lowest)]


def returned_pieces(pieces, offsets):
    near, *far = pieces
    return [near, *[swap(piece, offset) for piece, offset in zip(far, offsets)]]


def local_call(kernel, outputs, inputs, name):
    return pl.pallas_call(
        kernel,
        out_shape=outputs,
        in_specs=[VMEM] * len(inputs),
        out_specs=jax.tree.map(lambda _: VMEM, outputs),
        compiler_params=pltpu.CompilerParams(vmem_limit_bytes=VMEM_LIMIT),
        name=name,
    )(*inputs)


def add_bf16(pieces):
    total = sum((piece.astype(jnp.float32) for piece in pieces[1:]), pieces[0].astype(jnp.float32))
    return total.astype(jnp.bfloat16)


class Loader:
    def __init__(self, gate, up, down):
        self.experts = gate.shape[0]
        self.arrays = {"gate": gate, "up": up, "down": down}
        self.waiting = [
            (name, e, piece)
            for names in (("gate",),)
            for e in range(self.experts)
            for name in names
            for piece in range(PIECES)
        ]
        self.loaded = {}

    def take(self, count):
        taken, self.waiting = self.waiting[:count], self.waiting[count:]
        return taken

    def missing(self, expert, names):
        return sum(1 for name, e, _ in self.waiting if e == expert and name in names)

    def call(self, kernel, taken, inputs, specs, outputs, scratch, name, cost, **static):
        sources = [self.arrays[segment_name] for segment_name, _, _ in taken]
        shapes = [
            pltpu.VMEM((a.shape[1] // PIECES, a.shape[2]), a.dtype) for a in sources
        ]
        moved = sum(2 * math.prod(shape.shape) for shape in shapes)
        inputs = [
            pltpu.with_memory_space_constraint(x, pltpu.HBM) if spec is ANY else x
            for x, spec in zip(inputs, specs)
        ]
        sources = [pltpu.with_memory_space_constraint(x, pltpu.HBM) for x in sources]
        results = pl.pallas_call(
            functools.partial(kernel, places=tuple((e, p) for _, e, p in taken), **static),
            out_shape=tuple(outputs) + tuple(shapes),
            in_specs=list(specs) + [ANY] * len(taken),
            out_specs=tuple([VMEM] * (len(outputs) + len(taken))),
            scratch_shapes=list(scratch(len(taken))),
            compiler_params=pltpu.CompilerParams(vmem_limit_bytes=VMEM_LIMIT),
            cost_estimate=pl.CostEstimate(
                flops=0, bytes_accessed=cost + moved, transcendentals=0
            ),
            name=name,
        )(*inputs, *sources)
        for at, array in zip(taken, results[len(outputs) :]):
            self.loaded[at] = array
        return results[: len(outputs)]

    def pieces(self, name, expert):
        return [self.loaded[(name, expert, piece)] for piece in range(PIECES)]


def semaphores(count):
    return pltpu.SemaphoreType.DMA((max(count, 1),))


def load_more(loader, taken, after, scales):
    outputs = [jax.ShapeDtypeStruct(after.shape, after.dtype)]
    if scales:
        experts, depth, units = loader.arrays["gate"].shape
        columns = loader.arrays["down"].shape[2]
        outputs += [
            jax.ShapeDtypeStruct((experts, depth // QBLOCK, units), jnp.float32),
            jax.ShapeDtypeStruct((experts, depth // QBLOCK, units), jnp.float32),
            jax.ShapeDtypeStruct((experts, units // QBLOCK, columns), jnp.float32),
        ]
    return loader.call(
        load_kernel,
        taken,
        [after, *scales],
        [VMEM] * (1 + len(scales)),
        outputs,
        lambda count: [semaphores(count)],
        "load",
        1 << 20,
        spreading=1 if scales else 0,
    )


def per_device(
    residual,
    query,
    new_key,
    new_value,
    cache_key,
    cache_value,
    lengths,
    norm_gain,
    expert_ids,
    gate_levels,
    gate_codes,
    gate_scales,
    up_codes,
    up_scales,
    down_codes,
    down_scales,
):
    rows = residual.shape[0]
    half = D // 2
    extended = half + LANES
    experts, _, units = gate_codes.shape
    loader = Loader(gate_codes, up_codes, down_codes)
    inputs = [
        query,
        new_key,
        new_value,
        lengths,
        cache_key,
        cache_value,
        residual,
        norm_gain.reshape(1, D),
        expert_ids.T,
        gate_levels.T,
    ]
    scales = [
        gate_scales.transpose(1, 0, 2),
        up_scales.transpose(1, 0, 2),
        down_scales.transpose(2, 0, 1),
    ]
    stacked = pltpu.VMEM((KV_HEADS * SLOT, HEAD_DIM), jnp.float32)
    held = [
        (pltpu.SMEM if x.dtype == jnp.int32 else pltpu.VMEM)(x.shape, x.dtype) for x in inputs
    ]
    x, stream, *scales = loader.call(
        attend_kernel,
        loader.take(LOAD_ATTEND),
        inputs + scales,
        [ANY] * (len(inputs) + len(scales)),
        [
            jax.ShapeDtypeStruct((rows, D + LANES), jnp.bfloat16),
            jax.ShapeDtypeStruct((rows, D), jnp.float32),
            *[jax.ShapeDtypeStruct(table.shape, table.dtype) for table in scales],
        ],
        lambda count: held + [stacked] * 4 + [semaphores(13), semaphores(count)],
        "attend",
        4 << 20,
    )
    steps = rounds()
    spread_scales = None
    near, far = x, []
    for number, offsets in enumerate(steps):
        if far:
            near = jnp.concatenate([near, *far], axis=0)
        far = [swap(near, offset) for offset in offsets]
        taken = loader.take(LOAD_STEP[min(number, len(LOAD_STEP) - 1)])
        if spread_scales is None:
            near, *spread_scales = load_more(loader, taken, near, scales)
        elif taken:
            (near,) = load_more(loader, taken, near, [])
    gate_s, up_s, down_s = spread_scales
    count = (1 + len(far)) * near.shape[0]
    piece = jax.ShapeDtypeStruct((count, extended), jnp.bfloat16)
    kept, sent = local_call(split_kernel, (piece, piece), (near, *far), "split")
    other = swap(sent, None)
    parts = []
    before = other
    for e in range(experts):
        missing = loader.missing(e, ("gate",))
        if missing:
            (before,) = load_more(loader, loader.take(missing), before, [])
        (part,) = loader.call(
            gate_up_kernel,
            loader.take(LOAD_GATE_UP),
            [kept, before, gate_s, up_s, *loader.pieces("gate", e), up_codes],
            [VMEM] * (5 + PIECES),
            [jax.ShapeDtypeStruct((2 * count, 2 * units), jnp.bfloat16)],
            lambda loads: [semaphores(loads)],
            "gate_up",
            2 << 20,
            expert=e,
        )
        parts.append((part, swap(part, None)))
        before, _ = lax.optimization_barrier((before, part))
    carried = []
    for e in range(experts):
        last = e == experts - 1
        sums = jax.ShapeDtypeStruct((2 * count, half), jnp.float32)
        returned = jax.ShapeDtypeStruct((count, half), jnp.bfloat16)
        carried = loader.call(
            down_kernel,
            loader.take(LOAD_DOWN),
            [kept, other, *parts[e], down_s, down_codes, *carried],
            [VMEM] * (6 + len(carried)),
            [returned, returned] if last else [sums],
            lambda loads: [semaphores(loads)] + ([pltpu.VMEM(sums.shape, sums.dtype)] if last else []),
            "down",
            4 << 20,
            expert=e,
            experts=experts,
        )
    kept, sent = carried
    offsets = steps[-1]
    parts = 1 + len(offsets)
    piece = jax.ShapeDtypeStruct((count // parts, D), jnp.bfloat16)
    blocks = [0, *RETURN] if parts == 4 else list(range(parts))
    offsets = tuple(offsets[block - 1] for block in blocks[1:])
    joined = functools.partial(join_kernel, blocks=tuple(blocks))
    pieces = local_call(joined, (piece,) * parts, (kept, swap(sent, None)), "join")
    for following, _ in zip(reversed(steps[:-1]), steps[1:]):
        carried = add_bf16(returned_pieces(pieces, offsets))
        offsets = following
        pieces = jnp.split(carried, 1 + len(offsets))
    out = jax.ShapeDtypeStruct((rows, D), jnp.bfloat16)
    return local_call(finish_kernel, out, (stream, *returned_pieces(pieces, offsets)), "finish")


def solution(mesh):
    row = ("group", "role", "tp", "sub")
    in_specs = (
        P(row, None),
        P(row, None),
        P(row, None),
        P(row, None),
        P(row, None, None),
        P(row, None, None),
        P(row),
        P(),
        P(row, None),
        P(row, None),
        P("role", "sub", "tp"),
        P("role", "sub", "tp"),
        P("role", "sub", "tp"),
        P("role", "sub", "tp"),
        P("role", "tp", "sub"),
        P("role", "tp", "sub"),
    )
    return jax.shard_map(
        per_device, mesh=mesh, in_specs=in_specs, out_specs=P(row, None), check_vma=False
    )
```
